32 devices in a mesh: groups: 2 (over y), view: 4 (over z), col: 4 (over x, core).
Axes of the slice: x: 2, y: 2, z: 4, core: 2. Of those that a mesh axis runs over, the one named last changes fastest.
Arguments:
- volume: bfloat16 [2048, 512], P(('groups', 'view'), 'col'), parts along dimension 0, may hold values from -6 to 6
- requests: int32 [8, 4, 16], P(('groups', 'view')), parts along dimension 0, may hold values from 0 to 255, as said below
- counts: int32 [8, 4], P(('groups', 'view')), parts along dimension 0, may hold values from 1 to 16, as said below
- axial: bfloat16 [128, 4, 64], P('view'), may hold values from -0.75 to 0.75
- footprint: bfloat16 [128, 128, 1024], P('view', None, 'col'), may hold values from -0.5 to 0.5
- dual: bfloat16 [256, 4, 1024], P(('groups', 'view'), None, 'col'), parts along dimension 0, may hold values from -6 to 6
- measured: bfloat16 [256, 4, 1024], P(('groups', 'view'), None, 'col'), parts along dimension 0, may hold values from -6 to 6
- conv_first: bfloat16 [3, 3, 32, 3], replicated, may hold values from -1.25 to 1.25
- slopes_first: float32 [32], replicated, may hold values from 0.05 to 0.5
- conv_second: bfloat16 [3, 3, 32, 32], replicated, may hold values from -0.375 to 0.375
- slopes_second: float32 [32], replicated, may hold values from 0.05 to 0.5
- conv_last: bfloat16 [3, 3, 1, 32], replicated, may hold values from -0.375 to 0.375
Outputs:
- dual_out: bfloat16 [256, 4, 1024], P(('groups', 'view'), None, 'col'), parts along dimension 0
- backprojection: float32 [2048, 512], P(('groups', 'view'), 'col'), parts along dimension 0
The draws below stay inside these ranges and needn't reach their ends.
There are 2 independent parts, one for each index of `groups`. The reference program is written for one: setup_inputs(seed, part) draws one part's arguments, and reference() takes and returns one part's arrays. A program takes and returns all parts, laid end to end along the dimension named above; an argument that names none is the same for every part. Nothing has to cross between parts.
Inputs may be any that keep to these rules, and one draw needn't show every extreme that they name: Entry requests[o, g, s] names tile o * 256 + requests[o, g, s]; for each o and g the first counts[o, g] entries are distinct and the others are not used. `counts`: in every draw one view group takes 16 tiles from every owner.
All inputs are finite; a program needn't handle non-finite values.
Results may differ from the reference program's by a relative error of at most 0.0054.
Values may be sent and summed in bfloat16 or wider, within the bound.
No kernel may reach another device: no remote copies, remote signals or barrier semaphores. Data moves between devices by JAX's collectives and lax.ppermute only.
A program may use at most 128 MiB of HBM per device.

```python
import math
import jax
import jax.numpy as jnp
from jax import lax

TILE_DEV = 256
CAP = 16
VIEW_DEV = 32
UC = 256
ROWS = 4
CH = 32
TILE_VOX = 128
TILES = 1024
COLW = 512
VIEWS = 128
COLS = 1024
SLOTS = 64
N_VIEW = 4
N_COL = 4


def pick_row(row_key):
    return jax.random.permutation(row_key, TILE_DEV)[:CAP]


def draw_requests(key, part):
    key = jax.random.fold_in(key, 11)
    row_keys = jax.random.split(key, N_VIEW * N_VIEW)
    picks = jax.vmap(pick_row)(row_keys)
    return picks.reshape(N_VIEW, N_VIEW, CAP).astype(jnp.int32)


def draw_counts(key, part):
    key = jax.random.fold_in(key, 23)
    load_key, pick_key = jax.random.split(key)
    loads = jax.random.randint(load_key, (N_VIEW, N_VIEW), 1, CAP + 1)
    busiest = jax.random.randint(pick_key, (), 0, N_VIEW)
    chosen = jnp.arange(N_VIEW)[None, :] == busiest
    return jnp.where(chosen, CAP, loads).astype(jnp.int32)


def level_of(key, extent, cuts, least, high):
    def one(position, parts):
        steps = jax.random.uniform(jax.random.fold_in(jax.random.fold_in(key, 6), position), (parts,), jnp.float32, least / len(cuts), high / len(cuts))
        return jnp.repeat(jnp.exp(steps), extent[position] // parts).reshape((-1,) + (1,) * (len(extent) - position - 1))

    level = one(*cuts[0])
    for cut in cuts[1:]:
        level = level * one(*cut)
    return level


def normal_values(stream_key, shape, scale, reach, pieces=(), held_as=jnp.bfloat16):
    array = jax.random.normal(stream_key, shape, jnp.float32) * scale
    if len(pieces) > 0:
        array = level_of(stream_key, shape, pieces, -0.22, 0.18) * array
    return jnp.clip(array, min=-reach, max=reach).astype(held_as)


def setup_inputs(seed: int = 0, part: int = 0) -> dict:
    streams_of = jax.random.split(jax.random.key(seed), 13)
    own_keys = jax.random.split(jax.random.fold_in(streams_of[12], part), 13)
    volume = normal_values(own_keys[0], (TILES, COLW), 1.0, 6.0, ((0, 4), (1, 4)))
    requests = draw_requests(jax.random.fold_in(jax.random.fold_in(streams_of[12], part), 71), part)
    counts = draw_counts(jax.random.fold_in(jax.random.fold_in(streams_of[12], part), 71), part)
    axial = normal_values(streams_of[3], (VIEWS, ROWS, SLOTS), SLOTS ** -0.5, 0.75, ((0, 4),))
    footprint = normal_values(streams_of[4], (VIEWS, TILE_VOX, COLS), TILE_VOX ** -0.5, 0.5, ((0, 4), (2, 4)))
    dual = normal_values(own_keys[5], (VIEWS, ROWS, COLS), 1.0, 6.0, ((0, 4), (2, 4)))
    measured = normal_values(own_keys[6], (VIEWS, ROWS, COLS), 1.0, 6.0, ((0, 4), (2, 4)))
    conv_first = normal_values(streams_of[7], (3, 3, CH, 3), 27 ** -0.5, 1.25)
    slopes_first = jnp.clip(jnp.exp(jax.random.uniform(streams_of[8], (CH,), jnp.float32, math.log(0.05), math.log(0.5))), 0.05, 0.5)
    conv_second = normal_values(streams_of[9], (3, 3, CH, CH), (9 * CH) ** -0.5, 0.375)
    slopes_second = jnp.clip(jnp.exp(jax.random.uniform(streams_of[10], (CH,), jnp.float32, math.log(0.05), math.log(0.5))), 0.05, 0.5)
    conv_last = normal_values(streams_of[11], (3, 3, 1, CH), (9 * CH) ** -0.5, 0.375)
    return dict(volume=volume, requests=requests, counts=counts, axial=axial, footprint=footprint, dual=dual, measured=measured, conv_first=conv_first, slopes_first=slopes_first, conv_second=conv_second, slopes_second=slopes_second, conv_last=conv_last)


def conv_valid(padded, weights):
    rows_out = padded.shape[1] - 2
    cols_out = padded.shape[3] - 2
    summed = jnp.zeros((weights.shape[2], rows_out, padded.shape[2], cols_out), jnp.float32)
    for shift_v in range(3):
        for shift_u in range(3):
            window = padded[:, shift_v:shift_v + rows_out, :, shift_u:shift_u + cols_out].astype(jnp.float32)
            summed = summed + jnp.einsum('oc,cvrw->ovrw', weights[shift_v, shift_u].astype(jnp.float32), window)
    return summed


def wrap_views(field):
    return jnp.concatenate([field[:, -1:], field, field[:, :1]], axis=1)


def activate(values, slopes, col_start, col_limit):
    activated = jnp.where(values >= 0, values, slopes[:, None, None, None] * values)
    global_col = col_start + jnp.arange(values.shape[3], dtype=jnp.int32)
    inside = (global_col >= 0) & (global_col < col_limit)
    return jnp.where(inside[None, None, None, :], activated, jnp.zeros((), jnp.float32)).astype(jnp.bfloat16)


def reference(volume, requests, counts, axial, footprint, dual, measured, conv_first, slopes_first, conv_second, slopes_second, conv_last):
    owners = jnp.arange(N_VIEW, dtype=jnp.int32)
    tile_ids = owners[:, None, None] * TILE_DEV + requests
    in_use = jnp.arange(CAP, dtype=jnp.int32)[None, None, :] < counts[:, :, None]
    slot_ids = jnp.transpose(tile_ids, (1, 0, 2)).reshape(N_VIEW, SLOTS)
    slot_used = jnp.transpose(in_use, (1, 0, 2)).reshape(N_VIEW, SLOTS)
    axial_groups = axial.reshape(N_VIEW, VIEW_DEV, ROWS, SLOTS)
    foot_groups = footprint.reshape(N_VIEW, VIEW_DEV, TILE_VOX, COLS)

    def forward_group(inputs):
        ids, used, axial_part, foot_part = inputs
        gathered = jnp.where(used[:, None], volume[ids], jnp.zeros((), jnp.bfloat16))
        axial_sum = jnp.einsum('vrk,kc->vrc', axial_part.astype(jnp.float32), gathered.astype(jnp.float32)).astype(jnp.bfloat16)
        shaped = axial_sum.reshape(VIEW_DEV, ROWS, N_COL, TILE_VOX).astype(jnp.float32)
        foot_shaped = foot_part.reshape(VIEW_DEV, TILE_VOX, N_COL, UC).astype(jnp.float32)
        projected = jnp.einsum('vrjc,vcju->vrju', shaped, foot_shaped)
        return projected.reshape(VIEW_DEV, ROWS, COLS).astype(jnp.bfloat16)

    forward = lax.map(forward_group, (slot_ids, slot_used, axial_groups, foot_groups)).reshape(VIEWS, ROWS, COLS)
    stacked = jnp.stack([dual, forward, measured])
    widened = jnp.pad(stacked, ((0, 0), (0, 0), (0, 0), (3, 3)))

    def column_block(block_index):
        anchor = block_index * UC
        block = lax.dynamic_slice_in_dim(widened, anchor, UC + 6, 3)
        first_out = activate(conv_valid(wrap_views(block), conv_first), slopes_first, anchor - 2, COLS)
        second_out = activate(conv_valid(wrap_views(first_out), conv_second), slopes_second, anchor - 1, COLS)
        return conv_valid(wrap_views(second_out), conv_last)[0]

    updates = lax.map(column_block, jnp.arange(N_COL, dtype=jnp.int32))
    update = jnp.transpose(updates, (1, 2, 0, 3)).reshape(VIEWS, ROWS, COLS)
    dual_out = (dual.astype(jnp.float32) + update).astype(jnp.bfloat16)
    dual_groups = dual_out.reshape(N_VIEW, VIEW_DEV, ROWS, COLS)

    def back_group(inputs):
        dual_part, axial_part, foot_part = inputs
        dual_shaped = dual_part.reshape(VIEW_DEV, ROWS, N_COL, UC).astype(jnp.float32)
        foot_shaped = foot_part.reshape(VIEW_DEV, TILE_VOX, N_COL, UC).astype(jnp.float32)
        column_back = jnp.einsum('vrju,vcju->vrjc', dual_shaped, foot_shaped).reshape(VIEW_DEV, ROWS, COLW).astype(jnp.bfloat16)
        return jnp.einsum('vrk,vrc->kc', axial_part.astype(jnp.float32), column_back.astype(jnp.float32))

    partial_value = lax.map(back_group, (dual_groups, axial_groups, foot_groups))
    partial_value = jnp.where(slot_used[:, :, None], partial_value, jnp.zeros((), jnp.float32))
    backprojection = jax.ops.segment_sum(partial_value.reshape(N_VIEW * SLOTS, COLW), slot_ids.reshape(N_VIEW * SLOTS), num_segments=TILES)
    return dual_out, backprojection
```

```python
import functools

import jax
import jax.numpy as jnp
import numpy as np
from jax import lax
from jax.experimental import pallas as pl
from jax.experimental.pallas import tpu as pltpu
from jax.sharding import PartitionSpec as P

HALO = 3
BAND = 8
STEP = 6
LANES = 128
EDGE_ROWS = 16
VM = pl.BlockSpec(memory_space=pltpu.VMEM)
SM = pl.BlockSpec(memory_space=pltpu.SMEM)
F32 = jnp.float32
BF16 = jnp.bfloat16


def call(body, outs, scratch, args, specs=None, cost=None):
    single = not isinstance(outs, (list, tuple))
    return pl.pallas_call(
        body,
        out_shape=outs if single else list(outs),
        in_specs=specs or [VM] * len(args),
        out_specs=VM if single else [VM] * len(outs),
        scratch_shapes=scratch,
        compiler_params=pltpu.CompilerParams(vmem_limit_bytes=40 * 1024 * 1024),
        cost_estimate=cost and pl.CostEstimate(flops=cost[0], bytes_accessed=cost[1], transcendentals=0),
    )(*args)


def shape(dims, dtype=F32):
    return jax.ShapeDtypeStruct(dims, dtype)


def swap_perms(n):
    first = [(i, i ^ 1) for i in range(n)]
    second = [(i, (i + 1) % n if i % 2 else (i - 1) % n) for i in range(n)]
    return first, second


def both_ways(array_a, array_b, axis):
    first, second = swap_perms(lax.axis_size(axis))
    return lax.ppermute(array_a, axis, first), lax.ppermute(array_b, axis, second)


def exchange(pieces, axis):
    n = lax.axis_size(axis)
    if len(pieces) == 1:
        return [lax.all_to_all(pieces[0], axis, split_axis=0, concat_axis=0, tiled=True)]
    return [pieces[0]] + [lax.ppermute(pieces[k], axis, [(i, i ^ k) for i in range(n)]) for k in range(1, n)]


def gather_kernel(n, slots, split, req_ref, cnt_ref, vol_ref, *rest):
    outs, (vol_s, out_s) = rest[:-2], rest[-2:]
    tiles = vol_ref.shape[0]
    vol_s[0:tiles, :] = vol_ref[...].astype(F32)
    vol_s[tiles : tiles + 8, :] = jnp.zeros((8, vol_ref.shape[1]), F32)
    me = lax.axis_index("view")

    def chunk(k, dest):
        count = cnt_ref[0, dest]
        for s in range(slots):
            row = jnp.where(s < count, req_ref[0, dest, s], tiles)
            out_s[pl.ds(k * slots + s, 1), :] = vol_s[pl.ds(row, 1), :]

    if split:
        for k in range(n):
            chunk(k, me ^ k)
            outs[k][...] = out_s[k * slots : (k + 1) * slots, :].astype(BF16)
    else:
        lax.fori_loop(0, n, lambda k, c: (chunk(k, k), c)[1], 0)
        outs[0][...] = out_s[...].astype(BF16)


def scatter_kernel(n, slots, split, req_ref, cnt_ref, *rest):
    pieces, out_ref, acc = rest[:-2], rest[-2], rest[-1]
    tiles = out_ref.shape[0]
    acc[...] = jnp.zeros(acc.shape, F32)
    me = lax.axis_index("view")

    def chunk(source, dest):
        count = cnt_ref[0, dest]
        rows = [jnp.where(s < count, req_ref[0, dest, s], tiles) for s in range(slots)]
        sums = [acc[pl.ds(rows[s], 1), :] + source(s) for s in range(slots)]
        for s in range(slots):
            acc[pl.ds(rows[s], 1), :] = sums[s]

    if split:
        for k in range(n):
            chunk(lambda s: pieces[k][s : s + 1, :], me ^ k)
    else:
        lax.fori_loop(0, n, lambda k, c: (chunk(lambda s: pieces[0][pl.ds(k * slots + s, 1), :], k), c)[1], 0)
    out_ref[...] = acc[0:tiles, :]


def put_flat(flat_ref, start, block):
    for t in range(flat_ref.shape[0]):
        flat_ref[t, start : start + block.shape[0], :] = block[:, t * LANES : (t + 1) * LANES]


def widen(flat_ref, rows):
    tiles, both, _ = flat_ref.shape
    return jnp.concatenate(
        [flat_ref[t, pl.ds(r, both // rows, stride=rows), :] for r in range(rows) for t in range(tiles)], axis=1
    )


def widen_kernel(dual_ref, meas_ref, out_ref, flat):
    views, rows, _ = dual_ref.shape
    for i, ref in enumerate((dual_ref, meas_ref)):
        for v in range(views):
            put_flat(flat, v * rows, ref[v].astype(F32))
        out_ref[i] = widen(flat, rows)


def forward_kernel(n, rows, axial_ref, foot_ref, stat_ref, *rest):
    pieces, (fw_ref, a_ref, b_ref, slots_s, flat, edge) = rest[:-6], rest[-6:]
    me = lax.axis_index("view")
    views = foot_ref.shape[0]
    if len(pieces) > 1:
        cap = pieces[0].shape[0]
        for k in range(n):
            slots_s[pl.ds(pl.multiple_of((me ^ k) * cap, cap), cap), :] = pieces[k][...]
        slot_rows = slots_s[...]
    else:
        slot_rows = pieces[0][...]
    axial_sum = jnp.dot(axial_ref[...], slot_rows, preferred_element_type=F32).astype(BF16)
    per = 16 // rows
    owner = lax.broadcasted_iota(jnp.int32, (16, foot_ref.shape[2]), 0) // rows
    for q in range(views // per):
        lhs = axial_sum[16 * q : 16 * q + 16, :]
        got = None
        for i in range(per):
            one = jnp.dot(lhs, foot_ref[q * per + i], preferred_element_type=F32)
            got = one if got is None else jnp.where(owner == i, one, got)
        put_flat(flat, 16 * q, got.astype(BF16).astype(F32))
    fw = widen(flat, rows)
    fw_ref[...] = fw
    edge[...] = jnp.zeros(edge.shape, F32)
    for way, start in ((0, 0), (1, views - HALO)):
        for c in range(3):
            part = fw[start : start + HALO, :] if c == 1 else stat_ref[c // 2, start : start + HALO, :]
            edge[way, c * HALO : (c + 1) * HALO, :] = part
    even = me % 2 == 0
    to_prev, to_next = edge[0], edge[1]
    a_ref[...] = jnp.where(even, to_next, to_prev).astype(BF16)
    b_ref[...] = jnp.where(even, to_prev, to_next).astype(BF16)


def halo_of(a_ref, b_ref, channel):
    even = lax.axis_index("view") % 2 == 0
    rows = slice(channel * HALO, (channel + 1) * HALO)
    a = a_ref[...].astype(F32)[rows]
    b = b_ref[...].astype(F32)[rows]
    return jnp.where(even, b, a), jnp.where(even, a, b)


def lane(shape_):
    return lax.broadcasted_iota(jnp.int32, shape_, 1)


def strip_of(wide, rows, inner):
    cols = wide.shape[1] // rows
    at = lane((wide.shape[0], LANES))
    total = jnp.zeros((wide.shape[0], LANES), F32)
    for r in range(rows):
        head = wide[:, r * cols : r * cols + LANES]
        tail = wide[:, (r + 1) * cols - LANES : (r + 1) * cols]
        left, right = 16 * r, 64 + 16 * r
        if inner:
            picks = ((head, 0, left + HALO, 6), (tail, LANES - 6, right, 6))
        else:
            picks = ((tail, LANES - HALO, left, HALO), (head, 0, right + 6, HALO))
        for source, begin, target, width in picks:
            moved = pltpu.roll(source, (target - begin) % LANES, 1)
            total = jnp.where((at >= target) & (at < target + width), moved, total)
    return total


def own_strip_kernel(rows, fw_ref, stat_ref, in_ref, msg_ref):
    for c in range(3):
        wide = fw_ref[...] if c == 1 else stat_ref[c // 2]
        in_ref[c] = strip_of(wide, rows, True)
        msg_ref[c] = strip_of(wide, rows, False)


def strip_message_kernel(rows, in_ref, msg_ref, a_ref, b_ref, strip_ref, out_ref, buf):
    views = in_ref.shape[1]
    buf[...] = jnp.zeros(buf.shape, F32)
    strip_ref[...] = jnp.zeros(strip_ref.shape, F32)
    for c in range(3):
        for start, part in zip((0, HALO + views), halo_of(a_ref, b_ref, c)):
            strip_ref[c, start : start + HALO, :] = strip_of(part, rows, True)
            buf[c, start : start + HALO, :] = strip_of(part, rows, False)
        strip_ref[c, HALO : HALO + views, :] = in_ref[c]
        buf[c, HALO : HALO + views, :] = msg_ref[c]
        out_ref[c] = buf[c].astype(BF16)


def prelu(z, slopes_ref):
    channels = slopes_ref.shape[0]
    slopes = jnp.concatenate([slopes_ref[...]] * (z.shape[0] // channels), axis=0)
    slopes = jnp.concatenate([slopes] * (z.shape[1] // LANES), axis=1)
    return jnp.maximum(z, slopes * z)


def network(inputs, views, w1, w2, w3, a1, a2, s1, s2, s3, update, inside=None):
    n = s2.shape[2]
    channels = a1.shape[0]
    for c in range(3):
        x = inputs(c)
        s1[c] = pltpu.roll(x, 1, 1)
        s1[3 + c] = x
        s1[6 + c] = pltpu.roll(x, n - 1, 1)
    total = views + 4
    for k in range(-(-total // BAND)):
        m = min(BAND, total - BAND * k) * channels
        window = jnp.concatenate([s1[j, BAND * k : BAND * k + 16, :] for j in range(9)], axis=0).astype(BF16)
        z = prelu(jnp.dot(w1[0:m, :], window, preferred_element_type=F32), a1)
        if inside is not None:
            z = jnp.where(inside, z, 0.0)
        at = slice(BAND * k * channels, BAND * k * channels + m)
        s2[0, at, :] = pltpu.roll(z, 1, 1).astype(BF16)
        s2[1, at, :] = z.astype(BF16)
        s2[2, at, :] = pltpu.roll(z, n - 1, 1).astype(BF16)
    total = views + 2
    for k in range(-(-total // STEP)):
        count = min(STEP, total - STEP * k)
        m, depth = count * channels, (count + 2) * channels
        begin = STEP * k * channels
        if count == STEP:
            window = jnp.concatenate([s2[b, begin : begin + depth, :] for b in range(3)], axis=0)
            z = jnp.dot(w2[...], window, preferred_element_type=F32)
        else:
            full = (STEP + 2) * channels
            z = sum(
                jnp.dot(w2[0:m, b * full : b * full + depth], s2[b, begin : begin + depth, :], preferred_element_type=F32)
                for b in range(3)
            )
        z = prelu(z, a2)
        if inside is not None:
            z = jnp.where(inside, z, 0.0)
        s3[begin : begin + m, :] = z.astype(BF16)
    for k in range(-(-views // STEP)):
        count = min(STEP, views - STEP * k)
        depth = (count + 2) * channels
        begin = STEP * k * channels
        got = jnp.dot(w3[:, 0:depth], s3[begin : begin + depth, :], preferred_element_type=F32)
        out = pltpu.roll(got[0:8], 1, 1) + got[8:16] + pltpu.roll(got[16:24], n - 1, 1)
        update[STEP * k : STEP * k + count, :] = out[0:count, :]


def main_kernel(rows, fw_ref, stat_ref, ha_ref, hb_ref, w1, w2, w3, a1, a2, out_ref, x, s1, s2, s3, update):
    views = fw_ref.shape[0]
    x[...] = jnp.zeros(x.shape, F32)
    for c in range(3):
        before, after = halo_of(ha_ref, hb_ref, c)
        x[c, 0:HALO, :] = before
        x[c, HALO : HALO + views, :] = fw_ref[...] if c == 1 else stat_ref[c // 2]
        x[c, HALO + views : 2 * HALO + views, :] = after
    cols = fw_ref.shape[1] // rows
    for r in range(rows):
        at = slice(r * cols, (r + 1) * cols)
        network(lambda c: x[c, :, at], views, w1, w2, w3, a1, a2, s1, s2, s3, update)
        out_ref[:, at] = stat_ref[0, :, at] + update[...]


def back_kernel(
    n, rows, strip_ref, ra_ref, rb_ref, w1, w2, w3, a1, a2, main_ref, foot_ref, axial_ref, dual_ref, *rest
):
    parts, (x, s1, s2, s3, update, flat, back, part_s) = rest[:-8], rest[-8:]
    views, _, cols = foot_ref.shape[0], foot_ref.shape[1], foot_ref.shape[2]
    me, peers = lax.axis_index("col"), lax.axis_size("col")
    even = me % 2 == 0
    at = lane((1, LANES))
    left_side, step = at < 64, at % 16
    from_left = left_side & (step < HALO) & (me > 0)
    from_right = (~left_side) & (step >= 6) & (step < 9) & (me < peers - 1)
    inside = (left_side & ((step >= HALO) | (me > 0))) | ((~left_side) & ((step < 6) | (me < peers - 1)))
    for c in range(3):
        a, b = ra_ref[c].astype(F32), rb_ref[c].astype(F32)
        right = jnp.where(even, a, b)
        left = jnp.where(even, b, a)
        x[c] = jnp.where(from_left, left, jnp.where(from_right, right, strip_ref[c]))
    network(lambda c: x[c], views, w1, w2, w3, a1, a2, s1, s2, s3, update, inside)
    strip = x[0, HALO : HALO + views, :] + update[...]
    first = lane((views, LANES))
    for r in range(rows):
        head = main_ref[:, r * cols : r * cols + LANES]
        tail = main_ref[:, (r + 1) * cols - LANES : (r + 1) * cols]
        moved = pltpu.roll(strip, (-(16 * r + HALO)) % LANES, 1)
        head = jnp.where(first < HALO, moved, head)
        moved = pltpu.roll(strip, (LANES - HALO - (64 + 16 * r + HALO)) % LANES, 1)
        tail = jnp.where(first >= LANES - HALO, moved, tail)
        for t in range(cols // LANES):
            middle = main_ref[:, r * cols + t * LANES : r * cols + (t + 1) * LANES]
            last = cols // LANES - 1
            flat[t, pl.ds(r, views, stride=rows), :] = head if t == 0 else tail if t == last else middle
    per = 16 // rows
    owner = lax.broadcasted_iota(jnp.int32, (16, foot_ref.shape[1]), 0) // rows
    for q in range(views // per):
        block = jnp.concatenate([flat[t, 16 * q : 16 * q + 16, :] for t in range(cols // LANES)], axis=1).astype(BF16)
        dual_ref[16 * q : 16 * q + 16, :] = block
        got = None
        for i in range(per):
            one = lax.dot_general(
                block, foot_ref[q * per + i], (((1,), (1,)), ((), ())), preferred_element_type=F32
            )
            got = one if got is None else jnp.where(owner == i, one, got)
        back[16 * q : 16 * q + 16, :] = got.astype(BF16)
    partial = jnp.dot(axial_ref[...], back[...], preferred_element_type=F32)
    if len(parts) > 1:
        part_s[...] = partial
        cap = parts[0].shape[0]
        group = lax.axis_index("view")
        for k in range(n):
            parts[k][...] = part_s[pl.ds(pl.multiple_of((group ^ k) * cap, cap), cap), :]
    else:
        parts[0][...] = partial


def banded_weights(conv_first, conv_second, conv_last):
    channels = conv_second.shape[3]
    move = np.zeros((BAND, 3, 3, 3, 3, 3, 16), np.float32)
    for v in range(BAND):
        for a in range(3):
            for b in range(3):
                for c in range(3):
                    move[v, b, c, a, b, c, v + a] = 1.0
    move = jnp.asarray(move.reshape(BAND, 27, 144), BF16)
    first = conv_first.transpose(2, 1, 3, 0).reshape(channels, 27)
    w1 = jnp.einsum("ok,vkn->von", first, move, preferred_element_type=F32).astype(BF16)
    w1 = w1.reshape(BAND * channels, 144)

    def slide(w, steps):
        return jnp.stack(
            [
                jnp.pad(w, [(0, 0)] * (w.ndim - 1) + [(v * channels, (STEP - 1 - v) * channels)])
                for v in range(steps)
            ]
        )

    second = conv_second.transpose(1, 2, 0, 3).reshape(3, channels, 3 * channels)
    w2 = slide(second, STEP).transpose(0, 2, 1, 3).reshape(STEP * channels, 3 * (STEP + 2) * channels)
    last = conv_last.transpose(1, 2, 0, 3).reshape(3, 3 * channels)
    w3 = slide(last, STEP).transpose(1, 0, 2)
    w3 = jnp.pad(w3, ((0, 0), (0, 8 - STEP), (0, 0))).reshape(24, (STEP + 2) * channels)
    return w1, w2, w3


def shards(
    volume,
    requests,
    counts,
    axial,
    footprint,
    dual,
    measured,
    conv_first,
    slopes_first,
    conv_second,
    slopes_second,
    conv_last,
):
    n = lax.axis_size("view")
    slots = requests.shape[2]
    tiles, vox = volume.shape
    views, rows, cols = dual.shape
    wide = rows * cols
    channels = conv_second.shape[2]
    split = n in (2, 4)
    pieces = [shape((slots, vox), BF16)] * n if split else [shape((n * slots, vox), BF16)]
    outgoing = call(
        functools.partial(gather_kernel, n, slots, split),
        pieces,
        [pltpu.VMEM((tiles + 8, vox), F32), pltpu.VMEM((n * slots, vox), F32)],
        [requests, counts, volume],
        [SM, SM, VM],
    )
    incoming = exchange(outgoing, "view")

    stat = call(widen_kernel, shape((2, views, wide)), [pltpu.VMEM((cols // LANES, views * rows, LANES), F32)], [dual, measured])
    w1, w2, w3 = banded_weights(conv_first, conv_second, conv_last)
    a1 = jnp.broadcast_to(slopes_first[:, None], (channels, LANES))
    a2 = jnp.broadcast_to(slopes_second[:, None], (channels, LANES))
    axial_flat = axial.reshape(views * rows, n * slots)
    axial_back = axial_flat.T

    edge = shape((EDGE_ROWS, wide), BF16)
    fw, edge_a, edge_b = call(
        functools.partial(forward_kernel, n, rows),
        [shape((views, wide)), edge, edge],
        [
            pltpu.VMEM((n * slots, vox), BF16),
            pltpu.VMEM((cols // LANES, views * rows, LANES), F32),
            pltpu.VMEM((2, EDGE_ROWS, wide), F32),
        ],
        [axial_flat, footprint, stat, *incoming],
    )
    halo_a, halo_b = both_ways(edge_a, edge_b, "view")
    own = shape((3, views, LANES))
    strip_in, strip_msg = call(functools.partial(own_strip_kernel, rows), [own, own], [], [fw, stat])
    padded = 48
    strip, message = call(
        functools.partial(strip_message_kernel, rows),
        [shape((3, padded, LANES)), shape((3, padded, LANES), BF16)],
        [pltpu.VMEM((3, padded, LANES), F32)],
        [strip_in, strip_msg, halo_a, halo_b],
    )
    side_a, side_b = both_ways(message, message, "col")

    def net_scratch(width):
        return [
            pltpu.VMEM((9, padded, width), F32),
            pltpu.VMEM((3, (views + 4) * channels, width), BF16),
            pltpu.VMEM(((views + 2) * channels, width), BF16),
            pltpu.VMEM((views, width), F32),
        ]

    main = call(
        functools.partial(main_kernel, rows),
        shape((views, wide)),
        [pltpu.VMEM((3, padded, wide), F32), *net_scratch(cols)],
        [fw, stat, halo_a, halo_b, w1, w2, w3, a1, a2],
        cost=(2 * 10**9, 4 * 10**6),
    )
    parts = [shape((slots, vox))] * n if split else [shape((n * slots, vox))]
    dual_out, *returned = call(
        functools.partial(back_kernel, n, rows),
        [shape((views * rows, cols), BF16), *parts],
        [
            pltpu.VMEM((3, padded, LANES), F32),
            *net_scratch(LANES),
            pltpu.VMEM((cols // LANES, views * rows, LANES), F32),
            pltpu.VMEM((views * rows, vox), BF16),
            pltpu.VMEM((n * slots, vox), F32),
        ],
        [strip, side_a, side_b, w1, w2, w3, a1, a2, main, footprint, axial_back],
    )
    arrived = exchange(returned, "view")
    backprojection = call(
        functools.partial(scatter_kernel, n, slots, split),
        shape((tiles, vox)),
        [pltpu.VMEM((tiles + 8, vox), F32)],
        [requests, counts, *arrived],
        [SM, SM] + [VM] * len(arrived),
    )
    return dual_out.reshape(views, rows, cols), backprojection


def solution(mesh):
    in_specs = (
        P(("groups", "view"), "col"),
        P(("groups", "view"), None, None),
        P(("groups", "view"), None),
        P("view", None, None),
        P("view", None, "col"),
        P(("groups", "view"), None, "col"),
        P(("groups", "view"), None, "col"),
        P(),
        P(),
        P(),
        P(),
        P(),
    )
    out_specs = (P(("groups", "view"), None, "col"), P(("groups", "view"), "col"))
    return jax.shard_map(shards, mesh=mesh, in_specs=in_specs, out_specs=out_specs, check_vma=False)
```

```python
import functools

import jax
import jax.numpy as jnp
from jax import lax
from jax.experimental import pallas as pl
from jax.experimental.pallas import tpu as pltpu
from jax.sharding import PartitionSpec as P

HALO = 3
BAND = 8
STEP = 6
LANES = 128
VM = pl.BlockSpec(memory_space=pltpu.VMEM)
HBM = pl.BlockSpec(memory_space=pltpu.HBM)
F32 = jnp.float32
BF16 = jnp.bfloat16


def call(body, outs, scratch, args, specs=None, cost=None):
    single = not isinstance(outs, (list, tuple))
    return pl.pallas_call(
        body,
        out_shape=outs if single else list(outs),
        in_specs=specs or [VM] * len(args),
        out_specs=VM if single else [VM] * len(outs),
        scratch_shapes=scratch,
        compiler_params=pltpu.CompilerParams(vmem_limit_bytes=40 * 1024 * 1024),
        cost_estimate=cost and pl.CostEstimate(flops=cost[0], bytes_accessed=cost[1], transcendentals=0),
    )(*args)


def from_hbm(arrays):
    return [pltpu.with_memory_space_constraint(x, pltpu.HBM) for x in arrays]


def shape(dims, dtype=F32):
    return jax.ShapeDtypeStruct(dims, dtype)


def swap_perms(n):
    first = [(i, i ^ 1) for i in range(n)]
    second = [(i, (i + 1) % n if i % 2 else (i - 1) % n) for i in range(n)]
    return first, second


def both_ways(array_a, array_b, axis):
    first, second = swap_perms(lax.axis_size(axis))
    return lax.ppermute(array_a, axis, first), lax.ppermute(array_b, axis, second)


def exchange(pieces, axis):
    n = lax.axis_size(axis)
    if len(pieces) == 1:
        return [lax.all_to_all(pieces[0], axis, split_axis=0, concat_axis=0, tiled=True)]
    return [pieces[0]] + [lax.ppermute(pieces[k], axis, [(i, i ^ k) for i in range(n)]) for k in range(1, n)]


def iota(shape_, dim):
    return lax.broadcasted_iota(jnp.int32, shape_, dim)


def as_column(row):
    m = row.shape[1]
    spread = jnp.broadcast_to(row, (m, m))
    return jnp.sum(jnp.where(iota((m, m), 0) == iota((m, m), 1), spread, 0.0), axis=1, keepdims=True)


def wanted_row(req_ref, cnt_ref, dest):
    slots, n = req_ref.shape[2], cnt_ref.shape[1]
    row = req_ref[0, pl.ds(dest, 1), :].astype(F32)
    count = jnp.sum(jnp.where(iota((1, n), 1) == dest, cnt_ref[...].astype(F32), 0.0), axis=1, keepdims=True)
    return jnp.where(iota((1, slots), 1).astype(F32) < count, row, -1.0)


def fetch(pairs, sems):
    copies = [pltpu.make_async_copy(src, dst, sems.at[i]) for i, (src, dst) in enumerate(pairs)]
    for copy in copies:
        copy.start()
    return copies


def gather_kernel(n, slots, split, req_hbm, cnt_hbm, vol_hbm, *rest):
    outs, (req, cnt, vol, sems) = rest[:-4], rest[-4:]
    copies = fetch([(req_hbm, req), (cnt_hbm, cnt), (vol_hbm, vol)], sems)
    tiles = vol.shape[0]
    me = lax.axis_index("view")
    copies[0].wait()
    copies[1].wait()
    picks = []
    for k in range(n):
        column = as_column(wanted_row(req, cnt, me ^ k if split else k))
        hit = iota((slots, tiles), 1).astype(F32) == column
        picks.append(jnp.where(hit, 1.0, 0.0).astype(BF16))
    copies[2].wait()
    for k in range(n):
        got = jnp.dot(picks[k], vol[...], preferred_element_type=F32).astype(BF16)
        if split:
            outs[k][...] = got
        else:
            outs[0][k * slots : (k + 1) * slots, :] = got


def scatter_kernel(hot_ref, *rest):
    pieces, out_ref = rest[:-1], rest[-1]
    left = jnp.concatenate([p[...] for p in pieces], axis=0)
    total = None
    for _ in range(3):
        part = left.astype(BF16)
        left = left - part.astype(F32)
        got = jnp.dot(hot_ref[...], part, preferred_element_type=F32)
        total = got if total is None else total + got
    out_ref[...] = total


def put_flat(flat_ref, start, block):
    for t in range(flat_ref.shape[0]):
        flat_ref[t, start : start + block.shape[0], :] = block[:, t * LANES : (t + 1) * LANES]


def widen(flat_ref, rows):
    tiles, both, _ = flat_ref.shape
    return jnp.concatenate(
        [flat_ref[t, pl.ds(r, both // rows, stride=rows), :] for r in range(rows) for t in range(tiles)], axis=1
    )


def network_weights(first, second, last, w1_ref, w2_ref, w3_ref):
    channels = second.shape[3]
    sub, view = iota((16, BAND * channels), 0), iota((16, BAND * channels), 1) // channels
    blocks = []
    for b in range(3):
        for c in range(3):
            block = jnp.zeros(sub.shape, F32)
            for a in range(3):
                row = first[a, b].astype(F32)[c : c + 1, :]
                block = jnp.where(sub == view + a, jnp.concatenate([row] * BAND, axis=1), block)
            blocks.append(block)
    depth = 16 * len(blocks)
    blocks.append(jnp.zeros((-depth % LANES, BAND * channels), F32))
    w1_ref[...] = jnp.concatenate(blocks, axis=0).T[:, 0:depth].astype(BF16)
    full = (STEP + 2) * channels
    for b in range(3):
        taps = [second[a, b].astype(F32) for a in range(3)]
        wide = jnp.concatenate(taps + [jnp.zeros((channels, full - 3 * channels), F32)], axis=1)
        for v in range(STEP):
            at = slice(v * channels, (v + 1) * channels)
            w2_ref[at, b * full : (b + 1) * full] = pltpu.roll(wide, v * channels, 1).astype(BF16)
    out = []
    sub = iota((8, full), 0)
    for b in range(3):
        taps = [last[a].astype(F32)[b : b + 1, :] for a in range(3)]
        wide = jnp.concatenate(taps + [jnp.zeros((1, full - 3 * channels), F32)], axis=1)
        wide = jnp.broadcast_to(wide, (8, full))
        block = jnp.zeros((8, full), F32)
        for v in range(STEP):
            block = jnp.where(sub == v, pltpu.roll(wide, v * channels, 1), block)
        out.append(block)
    w3_ref[...] = jnp.concatenate(out, axis=0).astype(BF16)


def setup_kernel(n, split, *refs):
    ins, outs, (sems, flat, ax_flat), local = refs[:11], refs[11:21], refs[21:24], refs[24:]
    stat_ref, foot_ref, ax_ref, back_ref, w1_ref, w2_ref, w3_ref, a1_ref, a2_ref, hot_ref = outs
    dual, meas, axial, first, second, last, slopes_1, slopes_2, req, cnt = local
    copies = fetch(list(zip(ins, (*local, foot_ref))), sems)
    for copy in copies[:-1]:
        copy.wait()
    views, rows, slots = axial.shape
    for i, ref in enumerate((dual, meas)):
        for v in range(views):
            put_flat(flat, v * rows, ref[v].astype(F32))
        stat_ref[i] = widen(flat, rows)
    ax_flat[...] = jnp.zeros(ax_flat.shape, F32)
    for v in range(views):
        ax_flat[v * rows : (v + 1) * rows, 0:slots] = axial[v].astype(F32)
    ax_ref[...] = ax_flat[:, 0:slots].astype(BF16)
    back_ref[...] = ax_flat[...].T[0:slots, :].astype(BF16)
    network_weights(first, second, last, w1_ref, w2_ref, w3_ref)
    for ref, out in ((slopes_1, a1_ref), (slopes_2, a2_ref)):
        out[...] = jnp.broadcast_to(as_column(ref[...]), out.shape)
    me = lax.axis_index("view")
    row = jnp.concatenate([wanted_row(req, cnt, me ^ k if split else k) for k in range(n)], axis=1)
    hit = iota(hot_ref.shape, 0).astype(F32) == row
    hot_ref[...] = jnp.where(hit, 1.0, 0.0).astype(BF16)
    copies[-1].wait()


def forward_kernel(n, rows, axial_ref, foot_ref, stat_ref, *rest):
    pieces, (fw_ref, a_ref, b_ref, slots_s, flat, edge) = rest[:-6], rest[-6:]
    me = lax.axis_index("view")
    views = foot_ref.shape[0]
    if len(pieces) > 1:
        cap = pieces[0].shape[0]
        for k in range(n):
            slots_s[pl.ds(pl.multiple_of((me ^ k) * cap, cap), cap), :] = pieces[k][...]
        slot_rows = slots_s[...]
    else:
        slot_rows = pieces[0][...]
    axial_sum = jnp.dot(axial_ref[...], slot_rows, preferred_element_type=F32).astype(BF16)
    per = 16 // rows
    owner = lax.broadcasted_iota(jnp.int32, (16, foot_ref.shape[2]), 0) // rows
    for q in range(views // per):
        lhs = axial_sum[16 * q : 16 * q + 16, :]
        got = None
        for i in range(per):
            one = jnp.dot(lhs, foot_ref[q * per + i], preferred_element_type=F32)
            got = one if got is None else jnp.where(owner == i, one, got)
        put_flat(flat, 16 * q, got.astype(BF16).astype(F32))
    fw = widen(flat, rows)
    fw_ref[...] = fw
    edge[...] = jnp.zeros(edge.shape, F32)
    for way, start in ((0, 0), (1, views - HALO)):
        for c in range(3):
            part = fw[start : start + HALO, :] if c == 1 else stat_ref[c // 2, start : start + HALO, :]
            for t in range(part.shape[1] // LANES):
                at = (3 * t + c) * HALO
                edge[way, at : at + HALO, :] = part[:, t * LANES : (t + 1) * LANES]
    even = me % 2 == 0
    to_prev, to_next = edge[0], edge[1]
    a_ref[...] = jnp.where(even, to_next, to_prev).astype(BF16)
    b_ref[...] = jnp.where(even, to_prev, to_next).astype(BF16)


def sort_halo(a_ref, b_ref, halo):
    even = lax.axis_index("view") % 2 == 0
    a, b = a_ref[...].astype(F32), b_ref[...].astype(F32)
    halo[0] = jnp.where(even, b, a)
    halo[1] = jnp.where(even, a, b)


def halo_of(halo, way, channel, wide):
    starts = [(3 * t + channel) * HALO for t in range(wide // LANES)]
    return jnp.concatenate([halo[way, at : at + HALO, :] for at in starts], axis=1)


def strip_of(wide, rows, inner):
    cols = wide.shape[1] // rows
    at = iota((wide.shape[0], LANES), 1)
    total = jnp.zeros((wide.shape[0], LANES), F32)
    for r in range(rows):
        head = wide[:, r * cols : r * cols + LANES]
        tail = wide[:, (r + 1) * cols - LANES : (r + 1) * cols]
        left, right = 16 * r, 64 + 16 * r
        if inner:
            picks = ((head, 0, left + HALO, 6), (tail, LANES - 6, right, 6))
        else:
            picks = ((tail, LANES - HALO, left, HALO), (head, 0, right + 6, HALO))
        for source, begin, target, width in picks:
            moved = pltpu.roll(source, (target - begin) % LANES, 1)
            total = jnp.where((at >= target) & (at < target + width), moved, total)
    return total


def own_strip_kernel(rows, fw_ref, stat_ref, in_ref, msg_ref):
    for c in range(3):
        wide = fw_ref[...] if c == 1 else stat_ref[c // 2]
        in_ref[c] = strip_of(wide, rows, True)
        msg_ref[c] = strip_of(wide, rows, False)


def strip_message_kernel(rows, wide, in_ref, msg_ref, a_ref, b_ref, strip_ref, out_ref, buf, halo):
    views = in_ref.shape[1]
    sort_halo(a_ref, b_ref, halo)
    buf[...] = jnp.zeros(buf.shape, F32)
    strip_ref[...] = jnp.zeros(strip_ref.shape, F32)
    for c in range(3):
        for way, start in ((0, 0), (1, HALO + views)):
            part = halo_of(halo, way, c, wide)
            strip_ref[c, start : start + HALO, :] = strip_of(part, rows, True)
            buf[c, start : start + HALO, :] = strip_of(part, rows, False)
        strip_ref[c, HALO : HALO + views, :] = in_ref[c]
        buf[c, HALO : HALO + views, :] = msg_ref[c]
    total = buf[0] + pltpu.roll(buf[1], HALO, 1) + pltpu.roll(buf[2], 2 * HALO, 1)
    out_ref[...] = total.astype(BF16)


def prelu(z, slopes_ref):
    channels = slopes_ref.shape[0]
    slopes = jnp.concatenate([slopes_ref[...]] * (z.shape[0] // channels), axis=0)
    slopes = jnp.concatenate([slopes] * (z.shape[1] // LANES), axis=1)
    return jnp.maximum(z, slopes * z)


def network(inputs, views, w1, w2, w3, a1, a2, s1, s2, s3, update, inside=None):
    n = s2.shape[2]
    channels = a1.shape[0]
    for c in range(3):
        x = inputs(c)
        s1[c] = pltpu.roll(x, 1, 1)
        s1[3 + c] = x
        s1[6 + c] = pltpu.roll(x, n - 1, 1)
    total = views + 4
    for k in range(-(-total // BAND)):
        m = min(BAND, total - BAND * k) * channels
        window = jnp.concatenate([s1[j, BAND * k : BAND * k + 16, :] for j in range(9)], axis=0).astype(BF16)
        z = prelu(jnp.dot(w1[0:m, :], window, preferred_element_type=F32), a1)
        if inside is not None:
            z = jnp.where(inside, z, 0.0)
        at = slice(BAND * k * channels, BAND * k * channels + m)
        s2[0, at, :] = pltpu.roll(z, 1, 1).astype(BF16)
        s2[1, at, :] = z.astype(BF16)
        s2[2, at, :] = pltpu.roll(z, n - 1, 1).astype(BF16)
    total = views + 2
    for k in range(-(-total // STEP)):
        count = min(STEP, total - STEP * k)
        m, depth = count * channels, (count + 2) * channels
        begin = STEP * k * channels
        if count == STEP:
            window = jnp.concatenate([s2[b, begin : begin + depth, :] for b in range(3)], axis=0)
            z = jnp.dot(w2[...], window, preferred_element_type=F32)
        else:
            full = (STEP + 2) * channels
            z = sum(
                jnp.dot(w2[0:m, b * full : b * full + depth], s2[b, begin : begin + depth, :], preferred_element_type=F32)
                for b in range(3)
            )
        z = prelu(z, a2)
        if inside is not None:
            z = jnp.where(inside, z, 0.0)
        s3[begin : begin + m, :] = z.astype(BF16)
    for k in range(-(-views // STEP)):
        count = min(STEP, views - STEP * k)
        depth = (count + 2) * channels
        begin = STEP * k * channels
        got = jnp.dot(w3[:, 0:depth], s3[begin : begin + depth, :], preferred_element_type=F32)
        out = pltpu.roll(got[0:8], 1, 1) + got[8:16] + pltpu.roll(got[16:24], n - 1, 1)
        update[STEP * k : STEP * k + count, :] = out[0:count, :]


def main_kernel(rows, fw_ref, stat_ref, ha_ref, hb_ref, w1, w2, w3, a1, a2, out_ref, x, halo, s1, s2, s3, update):
    views, wide = fw_ref.shape
    sort_halo(ha_ref, hb_ref, halo)
    x[...] = jnp.zeros(x.shape, F32)
    for c in range(3):
        before, after = halo_of(halo, 0, c, wide), halo_of(halo, 1, c, wide)
        x[c, 0:HALO, :] = before
        x[c, HALO : HALO + views, :] = fw_ref[...] if c == 1 else stat_ref[c // 2]
        x[c, HALO + views : 2 * HALO + views, :] = after
    cols = fw_ref.shape[1] // rows
    for r in range(rows):
        at = slice(r * cols, (r + 1) * cols)
        network(lambda c: x[c, :, at], views, w1, w2, w3, a1, a2, s1, s2, s3, update)
        out_ref[:, at] = stat_ref[0, :, at] + update[...]


def back_kernel(
    n, rows, strip_ref, ra_ref, rb_ref, w1, w2, w3, a1, a2, main_ref, foot_ref, axial_ref, dual_ref, *rest
):
    parts, (x, s1, s2, s3, update, flat, back, part_s) = rest[:-8], rest[-8:]
    views, _, cols = foot_ref.shape[0], foot_ref.shape[1], foot_ref.shape[2]
    me, peers = lax.axis_index("col"), lax.axis_size("col")
    even = me % 2 == 0
    at = iota((1, LANES), 1)
    left_side, step = at < 64, at % 16
    from_left = left_side & (step < HALO) & (me > 0)
    from_right = (~left_side) & (step >= 6) & (step < 9) & (me < peers - 1)
    inside = (left_side & ((step >= HALO) | (me > 0))) | ((~left_side) & ((step < 6) | (me < peers - 1)))
    a, b = ra_ref[...].astype(F32), rb_ref[...].astype(F32)
    sides = jnp.where(at < 64, jnp.where(even, b, a), jnp.where(even, a, b))
    for c in range(3):
        side = pltpu.roll(sides, (-HALO * c) % LANES, 1)
        x[c] = jnp.where(from_left | from_right, side, strip_ref[c])
    network(lambda c: x[c], views, w1, w2, w3, a1, a2, s1, s2, s3, update, inside)
    strip = x[0, HALO : HALO + views, :] + update[...]
    first = iota((views, LANES), 1)
    for r in range(rows):
        head = main_ref[:, r * cols : r * cols + LANES]
        tail = main_ref[:, (r + 1) * cols - LANES : (r + 1) * cols]
        moved = pltpu.roll(strip, (-(16 * r + HALO)) % LANES, 1)
        head = jnp.where(first < HALO, moved, head)
        moved = pltpu.roll(strip, (LANES - HALO - (64 + 16 * r + HALO)) % LANES, 1)
        tail = jnp.where(first >= LANES - HALO, moved, tail)
        for t in range(cols // LANES):
            middle = main_ref[:, r * cols + t * LANES : r * cols + (t + 1) * LANES]
            last = cols // LANES - 1
            flat[t, pl.ds(r, views, stride=rows), :] = head if t == 0 else tail if t == last else middle
    per = 16 // rows
    owner = lax.broadcasted_iota(jnp.int32, (16, foot_ref.shape[1]), 0) // rows
    for q in range(views // per):
        block = jnp.concatenate([flat[t, 16 * q : 16 * q + 16, :] for t in range(cols // LANES)], axis=1).astype(BF16)
        dual_ref[16 * q : 16 * q + 16, :] = block
        got = None
        for i in range(per):
            one = lax.dot_general(
                block, foot_ref[q * per + i], (((1,), (1,)), ((), ())), preferred_element_type=F32
            )
            got = one if got is None else jnp.where(owner == i, one, got)
        back[16 * q : 16 * q + 16, :] = got.astype(BF16)
    partial = jnp.dot(axial_ref[...], back[...], preferred_element_type=F32)
    if len(parts) > 1:
        part_s[...] = partial
        cap = parts[0].shape[0]
        group = lax.axis_index("view")
        for k in range(n):
            parts[k][...] = part_s[pl.ds(pl.multiple_of((group ^ k) * cap, cap), cap), :]
    else:
        parts[0][...] = partial


def shards(
    volume,
    requests,
    counts,
    axial,
    footprint,
    dual,
    measured,
    conv_first,
    slopes_first,
    conv_second,
    slopes_second,
    conv_last,
):
    n = lax.axis_size("view")
    slots = requests.shape[2]
    tiles, vox = volume.shape
    views, rows, cols = dual.shape
    wide = rows * cols
    channels = conv_second.shape[2]
    split = n in (2, 4)
    dma = pltpu.SemaphoreType.DMA
    pieces = [shape((slots, vox), BF16)] * n if split else [shape((n * slots, vox), BF16)]
    outgoing = call(
        functools.partial(gather_kernel, n, slots, split),
        pieces,
        [
            pltpu.VMEM(requests.shape, jnp.int32),
            pltpu.VMEM(counts.shape, jnp.int32),
            pltpu.VMEM(volume.shape, BF16),
            dma((3,)),
        ],
        from_hbm([requests, counts, volume]),
        [HBM] * 3,
    )
    incoming = exchange(outgoing, "view")

    small = [
        dual,
        measured,
        axial,
        conv_first.transpose(0, 1, 3, 2),
        conv_second,
        conv_last.reshape(3, 3, channels),
        slopes_first.reshape(1, channels),
        slopes_second.reshape(1, channels),
        requests,
        counts,
    ]
    flat = pltpu.VMEM((cols // LANES, views * rows, LANES), F32)
    full = (STEP + 2) * channels
    stat, foot, axial_flat, axial_back, w1, w2, w3, a1, a2, hot = call(
        functools.partial(setup_kernel, n, split),
        [
            shape((2, views, wide)),
            shape(footprint.shape, BF16),
            shape((views * rows, n * slots), BF16),
            shape((n * slots, views * rows), BF16),
            shape((BAND * channels, 144), BF16),
            shape((STEP * channels, 3 * full), BF16),
            shape((24, full), BF16),
            shape((channels, LANES)),
            shape((channels, LANES)),
            shape((tiles, n * slots), BF16),
        ],
        [
            dma((len(small) + 1,)),
            flat,
            pltpu.VMEM((views * rows, -(-n * slots // LANES) * LANES), F32),
            *[pltpu.VMEM(x.shape, x.dtype) for x in small],
        ],
        from_hbm([*small, footprint]),
        [HBM] * (len(small) + 1),
        cost=(10**8, 4 * 10**6),
    )

    message_rows = -(-9 * (wide // LANES) // 16) * 16
    edge = shape((message_rows, LANES), BF16)
    halo = pltpu.VMEM((2, message_rows, LANES), F32)
    fw, edge_a, edge_b = call(
        functools.partial(forward_kernel, n, rows),
        [shape((views, wide)), edge, edge],
        [pltpu.VMEM((n * slots, vox), BF16), flat, halo],
        [axial_flat, foot, stat, *incoming],
    )
    halo_a, halo_b = both_ways(edge_a, edge_b, "view")
    own = shape((3, views, LANES))
    strip_in, strip_msg = call(
        functools.partial(own_strip_kernel, rows), [own, own], [], [fw, stat], cost=(10**7, 10**6)
    )
    padded = 48
    strip, message = call(
        functools.partial(strip_message_kernel, rows, wide),
        [shape((3, padded, LANES)), shape((padded, LANES), BF16)],
        [pltpu.VMEM((3, padded, LANES), F32), halo],
        [strip_in, strip_msg, halo_a, halo_b],
    )
    side_a, side_b = both_ways(message, message, "col")

    def net_scratch(width):
        return [
            pltpu.VMEM((9, padded, width), F32),
            pltpu.VMEM((3, (views + 4) * channels, width), BF16),
            pltpu.VMEM(((views + 2) * channels, width), BF16),
            pltpu.VMEM((views, width), F32),
        ]

    main = call(
        functools.partial(main_kernel, rows),
        shape((views, wide)),
        [pltpu.VMEM((3, padded, wide), F32), halo, *net_scratch(cols)],
        [fw, stat, halo_a, halo_b, w1, w2, w3, a1, a2],
        cost=(2 * 10**9, 4 * 10**6),
    )
    parts = [shape((slots, vox))] * n if split else [shape((n * slots, vox))]
    dual_out, *returned = call(
        functools.partial(back_kernel, n, rows),
        [shape((views * rows, cols), BF16), *parts],
        [
            pltpu.VMEM((3, padded, LANES), F32),
            *net_scratch(LANES),
            flat,
            pltpu.VMEM((views * rows, vox), BF16),
            pltpu.VMEM((n * slots, vox), F32),
        ],
        [strip, side_a, side_b, w1, w2, w3, a1, a2, main, foot, axial_back],
    )
    arrived = exchange(returned, "view")
    backprojection = call(scatter_kernel, shape((tiles, vox)), [], [hot, *arrived])
    return dual_out.reshape(views, rows, cols), backprojection


def solution(mesh):
    in_specs = (
        P(("groups", "view"), "col"),
        P(("groups", "view"), None, None),
        P(("groups", "view"), None),
        P("view", None, None),
        P("view", None, "col"),
        P(("groups", "view"), None, "col"),
        P(("groups", "view"), None, "col"),
        P(),
        P(),
        P(),
        P(),
        P(),
    )
    out_specs = (P(("groups", "view"), None, "col"), P(("groups", "view"), "col"))
    return jax.shard_map(shards, mesh=mesh, in_specs=in_specs, out_specs=out_specs, check_vma=False)
```

```python
import functools

import jax
import jax.numpy as jnp
from jax import lax
from jax.experimental import pallas as pl
from jax.experimental.pallas import tpu as pltpu
from jax.sharding import PartitionSpec as P

HALO = 3
BAND = 8
STEP = 6
LANES = 128
VM = pl.BlockSpec(memory_space=pltpu.VMEM)
HBM = pl.BlockSpec(memory_space=pltpu.HBM)
F32 = jnp.float32
BF16 = jnp.bfloat16


def call(body, outs, scratch, args, specs=None, cost=None):
    single = not isinstance(outs, (list, tuple))
    return pl.pallas_call(
        body,
        out_shape=outs if single else list(outs),
        in_specs=specs or [VM] * len(args),
        out_specs=VM if single else [VM] * len(outs),
        scratch_shapes=scratch,
        compiler_params=pltpu.CompilerParams(vmem_limit_bytes=40 * 1024 * 1024),
        cost_estimate=cost and pl.CostEstimate(flops=cost[0], bytes_accessed=cost[1], transcendentals=0),
    )(*args)


def from_hbm(arrays):
    return [pltpu.with_memory_space_constraint(x, pltpu.HBM) for x in arrays]


def shape(dims, dtype=F32):
    return jax.ShapeDtypeStruct(dims, dtype)


def swap_perms(n):
    first = [(i, i ^ 1) for i in range(n)]
    second = [(i, (i + 1) % n if i % 2 else (i - 1) % n) for i in range(n)]
    return first, second


def both_ways(array_a, array_b, axis):
    first, second = swap_perms(lax.axis_size(axis))
    return lax.ppermute(array_a, axis, first), lax.ppermute(array_b, axis, second)


def order(n):
    return [0] + [k for k in (2, 3, 1) if k < n]


def partner(n, split, k):
    return lax.axis_index("view") ^ order(n)[k] if split else k


def exchange(pieces, axis):
    n = lax.axis_size(axis)
    if len(pieces) == 1:
        return [lax.all_to_all(pieces[0], axis, split_axis=0, concat_axis=0, tiled=True)]
    first, *others = pieces
    return [first] + [lax.ppermute(p, axis, [(i, i ^ k) for i in range(n)]) for p, k in zip(others, order(n)[1:])]


def iota(shape_, dim):
    return lax.broadcasted_iota(jnp.int32, shape_, dim)


def as_column(row):
    m = row.shape[1]
    spread = jnp.broadcast_to(row, (m, m))
    return jnp.sum(jnp.where(iota((m, m), 0) == iota((m, m), 1), spread, 0.0), axis=1, keepdims=True)


def wanted_row(req_ref, cnt_ref, dest):
    slots, n = req_ref.shape[2], cnt_ref.shape[1]
    row = req_ref[0, pl.ds(dest, 1), :].astype(F32)
    count = jnp.sum(jnp.where(iota((1, n), 1) == dest, cnt_ref[...].astype(F32), 0.0), axis=1, keepdims=True)
    return jnp.where(iota((1, slots), 1).astype(F32) < count, row, -1.0)


def fetch(pairs, sems):
    copies = [pltpu.make_async_copy(src, dst, sems.at[i]) for i, (src, dst) in enumerate(pairs)]
    for copy in copies:
        copy.start()
    return copies


def gather_kernel(n, slots, split, req_hbm, cnt_hbm, vol_hbm, *rest):
    outs, (req, cnt, vol, sems) = rest[:-4], rest[-4:]
    copies = fetch([(req_hbm, req), (cnt_hbm, cnt), (vol_hbm, vol)], sems)
    tiles = vol.shape[0]
    copies[0].wait()
    copies[1].wait()
    picks = []
    for k in range(n):
        column = as_column(wanted_row(req, cnt, partner(n, split, k)))
        hit = iota((slots, tiles), 1).astype(F32) == column
        picks.append(jnp.where(hit, 1.0, 0.0).astype(BF16))
    copies[2].wait()
    for k in range(n):
        got = jnp.dot(picks[k], vol[...], preferred_element_type=F32).astype(BF16)
        if split:
            outs[k][...] = got
        else:
            outs[0][k * slots : (k + 1) * slots, :] = got


def scatter_kernel(hot_ref, *rest):
    pieces, out_ref = rest[:-1], rest[-1]
    left = jnp.concatenate([p[...] for p in pieces], axis=0)
    total = None
    for _ in range(3):
        part = left.astype(BF16)
        left = left - part.astype(F32)
        got = jnp.dot(hot_ref[...], part, preferred_element_type=F32)
        total = got if total is None else total + got
    out_ref[...] = total


def put_flat(flat_ref, start, block):
    for t in range(flat_ref.shape[0]):
        flat_ref[t, start : start + block.shape[0], :] = block[:, t * LANES : (t + 1) * LANES]


def widen(flat_ref, rows):
    tiles, both, _ = flat_ref.shape
    return jnp.concatenate(
        [flat_ref[t, pl.ds(r, both // rows, stride=rows), :] for r in range(rows) for t in range(tiles)], axis=1
    )


def network_weights(first, second, last, w1_ref, w2_ref, w3_ref):
    channels = second.shape[3]
    sub, view = iota((16, BAND * channels), 0), iota((16, BAND * channels), 1) // channels
    blocks = []
    for b in range(3):
        for c in range(3):
            block = jnp.zeros(sub.shape, F32)
            for a in range(3):
                row = first[a, b].astype(F32)[c : c + 1, :]
                block = jnp.where(sub == view + a, jnp.concatenate([row] * BAND, axis=1), block)
            blocks.append(block)
    depth = 16 * len(blocks)
    blocks.append(jnp.zeros((-depth % LANES, BAND * channels), F32))
    w1_ref[...] = jnp.concatenate(blocks, axis=0).T[:, 0:depth].astype(BF16)
    full = (STEP + 2) * channels
    for b in range(3):
        taps = [second[a, b].astype(F32) for a in range(3)]
        wide = jnp.concatenate(taps + [jnp.zeros((channels, full - 3 * channels), F32)], axis=1)
        for v in range(STEP):
            at = slice(v * channels, (v + 1) * channels)
            w2_ref[at, b * full : (b + 1) * full] = pltpu.roll(wide, v * channels, 1).astype(BF16)
    out = []
    sub = iota((8, full), 0)
    for b in range(3):
        taps = [last[a].astype(F32)[b : b + 1, :] for a in range(3)]
        wide = jnp.concatenate(taps + [jnp.zeros((1, full - 3 * channels), F32)], axis=1)
        wide = jnp.broadcast_to(wide, (8, full))
        block = jnp.zeros((8, full), F32)
        for v in range(STEP):
            block = jnp.where(sub == v, pltpu.roll(wide, v * channels, 1), block)
        out.append(block)
    w3_ref[...] = jnp.concatenate(out, axis=0).astype(BF16)


def setup_kernel(n, split, *refs):
    ins, outs, (sems, flat, ax_flat), local = refs[:11], refs[11:21], refs[21:24], refs[24:]
    stat_ref, foot_ref, ax_ref, back_ref, w1_ref, w2_ref, w3_ref, a1_ref, a2_ref, hot_ref = outs
    dual, meas, axial, first, second, last, slopes_1, slopes_2, req, cnt = local
    copies = fetch(list(zip(ins, (*local, foot_ref))), sems)
    for copy in copies[:-1]:
        copy.wait()
    views, rows, slots = axial.shape
    for i, ref in enumerate((dual, meas)):
        for v in range(views):
            put_flat(flat, v * rows, ref[v].astype(F32))
        stat_ref[i] = widen(flat, rows)
    ax_flat[...] = jnp.zeros(ax_flat.shape, F32)
    for v in range(views):
        ax_flat[v * rows : (v + 1) * rows, 0:slots] = axial[v].astype(F32)
    ax_ref[...] = ax_flat[:, 0:slots].astype(BF16)
    back_ref[...] = ax_flat[...].T[0:slots, :].astype(BF16)
    network_weights(first, second, last, w1_ref, w2_ref, w3_ref)
    for ref, out in ((slopes_1, a1_ref), (slopes_2, a2_ref)):
        out[...] = jnp.broadcast_to(as_column(ref[...]), out.shape)
    row = jnp.concatenate([wanted_row(req, cnt, partner(n, split, k)) for k in range(n)], axis=1)
    hit = iota(hot_ref.shape, 0).astype(F32) == row
    hot_ref[...] = jnp.where(hit, 1.0, 0.0).astype(BF16)
    copies[-1].wait()


def forward_kernel(n, rows, axial_ref, foot_ref, stat_ref, *rest):
    pieces, (fw_ref, a_ref, b_ref, slots_s, flat, edge) = rest[:-6], rest[-6:]
    me = lax.axis_index("view")
    views = foot_ref.shape[0]
    if len(pieces) > 1:
        cap = pieces[0].shape[0]
        for k in range(n):
            slots_s[pl.ds(pl.multiple_of(partner(n, True, k) * cap, cap), cap), :] = pieces[k][...]
        slot_rows = slots_s[...]
    else:
        slot_rows = pieces[0][...]
    axial_sum = jnp.dot(axial_ref[...], slot_rows, preferred_element_type=F32).astype(BF16)
    per = 16 // rows
    owner = lax.broadcasted_iota(jnp.int32, (16, foot_ref.shape[2]), 0) // rows
    for q in range(views // per):
        lhs = axial_sum[16 * q : 16 * q + 16, :]
        got = None
        for i in range(per):
            one = jnp.dot(lhs, foot_ref[q * per + i], preferred_element_type=F32)
            got = one if got is None else jnp.where(owner == i, one, got)
        put_flat(flat, 16 * q, got.astype(BF16).astype(F32))
    fw = widen(flat, rows)
    fw_ref[...] = fw
    edge[...] = jnp.zeros(edge.shape, F32)
    for way, start in ((0, 0), (1, views - HALO)):
        for c in range(3):
            part = fw[start : start + HALO, :] if c == 1 else stat_ref[c // 2, start : start + HALO, :]
            for t in range(part.shape[1] // LANES):
                at = (3 * t + c) * HALO
                edge[way, at : at + HALO, :] = part[:, t * LANES : (t + 1) * LANES]
    even = me % 2 == 0
    to_prev, to_next = edge[0], edge[1]
    a_ref[...] = jnp.where(even, to_next, to_prev).astype(BF16)
    b_ref[...] = jnp.where(even, to_prev, to_next).astype(BF16)


def sort_halo(a_ref, b_ref, halo):
    even = lax.axis_index("view") % 2 == 0
    a, b = a_ref[...].astype(F32), b_ref[...].astype(F32)
    halo[0] = jnp.where(even, b, a)
    halo[1] = jnp.where(even, a, b)


def halo_of(halo, way, channel, wide):
    starts = [(3 * t + channel) * HALO for t in range(wide // LANES)]
    return jnp.concatenate([halo[way, at : at + HALO, :] for at in starts], axis=1)


def strip_of(wide, rows, inner):
    cols = wide.shape[1] // rows
    at = iota((wide.shape[0], LANES), 1)
    total = jnp.zeros((wide.shape[0], LANES), F32)
    for r in range(rows):
        head = wide[:, r * cols : r * cols + LANES]
        tail = wide[:, (r + 1) * cols - LANES : (r + 1) * cols]
        left, right = 16 * r, 64 + 16 * r
        if inner:
            picks = ((head, 0, left + HALO, 6), (tail, LANES - 6, right, 6))
        else:
            picks = ((tail, LANES - HALO, left, HALO), (head, 0, right + 6, HALO))
        for source, begin, target, width in picks:
            moved = pltpu.roll(source, (target - begin) % LANES, 1)
            total = jnp.where((at >= target) & (at < target + width), moved, total)
    return total


def own_strip_kernel(rows, fw_ref, stat_ref, in_ref, msg_ref):
    for c in range(3):
        wide = fw_ref[...] if c == 1 else stat_ref[c // 2]
        in_ref[c] = strip_of(wide, rows, True)
        msg_ref[c] = strip_of(wide, rows, False)


def strip_message_kernel(rows, wide, in_ref, msg_ref, a_ref, b_ref, strip_ref, out_ref, buf, halo):
    views = in_ref.shape[1]
    sort_halo(a_ref, b_ref, halo)
    buf[...] = jnp.zeros(buf.shape, F32)
    strip_ref[...] = jnp.zeros(strip_ref.shape, F32)
    for c in range(3):
        for way, start in ((0, 0), (1, HALO + views)):
            part = halo_of(halo, way, c, wide)
            strip_ref[c, start : start + HALO, :] = strip_of(part, rows, True)
            buf[c, start : start + HALO, :] = strip_of(part, rows, False)
        strip_ref[c, HALO : HALO + views, :] = in_ref[c]
        buf[c, HALO : HALO + views, :] = msg_ref[c]
    total = buf[0] + pltpu.roll(buf[1], HALO, 1) + pltpu.roll(buf[2], 2 * HALO, 1)
    out_ref[...] = total.astype(BF16)


def prelu(z, slopes_ref):
    channels = slopes_ref.shape[0]
    slopes = jnp.concatenate([slopes_ref[...]] * (z.shape[0] // channels), axis=0)
    slopes = jnp.concatenate([slopes] * (z.shape[1] // LANES), axis=1)
    return jnp.maximum(z, slopes * z)


def shifted(z):
    return pltpu.roll(z, 1, 1), z, pltpu.roll(z, z.shape[1] - 1, 1)


def chunks(ref):
    n = ref.shape[-1]
    width = min(n, 2 * LANES)
    return [slice(i, i + width) for i in range(0, n, width)]


def first_layer(inputs, count, w1, a1, s1, s2, base=0, inside=None):
    channels = a1.shape[0]
    for at in chunks(s2):
        for c in range(3):
            for b, x in enumerate(shifted(inputs(c, at))):
                s1[3 * b + c, :, at] = x
    for k in range(-(-count // BAND)):
        for at in chunks(s2):
            m = min(BAND, count - BAND * k) * channels
            window = jnp.concatenate([s1[j, BAND * k : BAND * k + 16, at] for j in range(9)], axis=0).astype(BF16)
            z = prelu(jnp.dot(w1[0:m, :], window, preferred_element_type=F32), a1)
            if inside is not None:
                z = jnp.where(inside, z, 0.0)
            row = base + BAND * k * channels
            for b, x in enumerate(shifted(z)):
                s2[b, row : row + m, at] = x.astype(BF16)


def second_layer(count, w2, a2, s2, s3, base=0, inside=None):
    channels = a2.shape[0]
    full = (STEP + 2) * channels
    for k in range(-(-count // STEP)):
        part = min(STEP, count - STEP * k)
        m, depth = part * channels, (part + 2) * channels
        begin = STEP * k * channels
        for at in chunks(s2):
            windows = [s2[b, begin : begin + depth, at] for b in range(3)]
            if part == STEP:
                z = jnp.dot(w2[...], jnp.concatenate(windows, axis=0), preferred_element_type=F32)
            else:
                z = sum(
                    jnp.dot(w2[0:m, b * full : b * full + depth], windows[b], preferred_element_type=F32) for b in range(3)
                )
            z = prelu(z, a2)
            if inside is not None:
                z = jnp.where(inside, z, 0.0)
            s3[base + begin : base + begin + m, at] = z.astype(BF16)


def last_layer(count, channels, w3, s3, update):
    for k in range(-(-count // STEP)):
        part = min(STEP, count - STEP * k)
        begin, depth = STEP * k * channels, (part + 2) * channels
        for at in chunks(s3):
            got = jnp.dot(w3[:, 0:depth], s3[begin : begin + depth, at], preferred_element_type=F32)
            n = got.shape[1]
            out = pltpu.roll(got[0:8], 1, 1) + got[8:16] + pltpu.roll(got[16:24], n - 1, 1)
            update[STEP * k : STEP * k + part, at] = out[0:part, :]


def inner_kernel(fw_ref, stat_ref, w1, w2, w3, a1, a2, out_ref, one_ref, two_ref, x, s1, s2, s3, update):
    views = fw_ref.shape[0]
    channels = a1.shape[0]
    x[...] = jnp.zeros(x.shape, F32)
    for c in range(3):
        x[c, 0:views, :] = fw_ref[...] if c == 1 else stat_ref[c // 2]
    first_layer(lambda c, at: x[c, :, at], views - 2, w1, a1, s1, s2)
    second_layer(views - 4, w2, a2, s2, s3)
    last_layer(views - 6, channels, w3, s3, update)
    out_ref[HALO : views - HALO, :] = stat_ref[0, HALO : views - HALO, :] + update[...]
    two = 2 * channels
    for ref, ends in ((one_ref, s2.at[1]), (two_ref, s3)):
        end = ends.shape[0]
        ref[0:two, :] = ends[0:two, :]
        ref[two : 2 * two, :] = ends[end - two : end, :]


def outer_kernel(
    fw_ref, stat_ref, ha_ref, hb_ref, in_ref, one_ref, two_ref, w1, w2, w3, a1, a2, out_ref, x, halo, s1, s2, s3, update
):
    views, wide = fw_ref.shape
    channels = a1.shape[0]
    sort_halo(ha_ref, hb_ref, halo)
    x[...] = jnp.zeros(x.shape, F32)
    for c in range(3):
        x[0, c, 0:HALO, :] = halo_of(halo, 0, c, wide)
        x[1, c, 2 : 2 + HALO, :] = halo_of(halo, 1, c, wide)
        source = fw_ref if c == 1 else stat_ref.at[c // 2]
        x[0, c, HALO : HALO + 2, :] = source[0:2, :]
        x[1, c, 0:2, :] = source[views - 2 : views, :]
    two = 2 * channels
    new, old = (0, two), (HALO * channels, 0)
    for side in range(2):
        kept = slice(side * two, (side + 1) * two)
        for at in chunks(one_ref):
            for b, moved in enumerate(shifted(one_ref[kept, at].astype(F32))):
                s2[side, b, old[side] : old[side] + two, at] = moved.astype(BF16)
        s3[side, old[side] : old[side] + two, :] = two_ref[kept, :]
    for side in range(2):
        first_layer(lambda c, at: x[side, c, :, at], HALO, w1, a1, s1.at[side], s2.at[side], new[side])
    for side in range(2):
        second_layer(HALO, w2, a2, s2.at[side], s3.at[side], new[side])
    for side in range(2):
        last_layer(HALO, channels, w3, s3.at[side], update.at[side])
    out_ref[HALO : views - HALO, :] = in_ref[HALO : views - HALO, :]
    for side, begin in ((0, 0), (1, views - HALO)):
        out_ref[begin : begin + HALO, :] = stat_ref[0, begin : begin + HALO, :] + update[side]


def back_kernel(
    n, rows, strip_ref, ra_ref, rb_ref, w1, w2, w3, a1, a2, main_ref, foot_ref, axial_ref, dual_ref, *rest
):
    parts, (x, s1, s2, s3, update, flat, back, part_s) = rest[:-8], rest[-8:]
    views, _, cols = foot_ref.shape[0], foot_ref.shape[1], foot_ref.shape[2]
    me, peers = lax.axis_index("col"), lax.axis_size("col")
    even = me % 2 == 0
    at = iota((1, LANES), 1)
    left_side, step = at < 64, at % 16
    from_left = left_side & (step < HALO) & (me > 0)
    from_right = (~left_side) & (step >= 6) & (step < 9) & (me < peers - 1)
    inside = (left_side & ((step >= HALO) | (me > 0))) | ((~left_side) & ((step < 6) | (me < peers - 1)))
    a, b = ra_ref[...].astype(F32), rb_ref[...].astype(F32)
    sides = jnp.where(at < 64, jnp.where(even, b, a), jnp.where(even, a, b))
    for c in range(3):
        side = pltpu.roll(sides, (-HALO * c) % LANES, 1)
        x[c] = jnp.where(from_left | from_right, side, strip_ref[c])
    first_layer(lambda c, at: x[c, :, at], views + 4, w1, a1, s1, s2, 0, inside)
    second_layer(views + 2, w2, a2, s2, s3, 0, inside)
    last_layer(views, a1.shape[0], w3, s3, update)
    strip = x[0, HALO : HALO + views, :] + update[...]
    first = iota((views, LANES), 1)
    for r in range(rows):
        head = main_ref[:, r * cols : r * cols + LANES]
        tail = main_ref[:, (r + 1) * cols - LANES : (r + 1) * cols]
        moved = pltpu.roll(strip, (-(16 * r + HALO)) % LANES, 1)
        head = jnp.where(first < HALO, moved, head)
        moved = pltpu.roll(strip, (LANES - HALO - (64 + 16 * r + HALO)) % LANES, 1)
        tail = jnp.where(first >= LANES - HALO, moved, tail)
        for t in range(cols // LANES):
            middle = main_ref[:, r * cols + t * LANES : r * cols + (t + 1) * LANES]
            last = cols // LANES - 1
            flat[t, pl.ds(r, views, stride=rows), :] = head if t == 0 else tail if t == last else middle
    per = 16 // rows
    owner = lax.broadcasted_iota(jnp.int32, (16, foot_ref.shape[1]), 0) // rows
    for q in range(views // per):
        block = jnp.concatenate([flat[t, 16 * q : 16 * q + 16, :] for t in range(cols // LANES)], axis=1).astype(BF16)
        dual_ref[16 * q : 16 * q + 16, :] = block
        got = None
        for i in range(per):
            one = lax.dot_general(
                block, foot_ref[q * per + i], (((1,), (1,)), ((), ())), preferred_element_type=F32
            )
            got = one if got is None else jnp.where(owner == i, one, got)
        back[16 * q : 16 * q + 16, :] = got.astype(BF16)
    partial = jnp.dot(axial_ref[...], back[...], preferred_element_type=F32)
    if len(parts) > 1:
        part_s[...] = partial
        cap = parts[0].shape[0]
        for k in range(n):
            parts[k][...] = part_s[pl.ds(pl.multiple_of(partner(n, True, k) * cap, cap), cap), :]
    else:
        parts[0][...] = partial


def shards(
    volume,
    requests,
    counts,
    axial,
    footprint,
    dual,
    measured,
    conv_first,
    slopes_first,
    conv_second,
    slopes_second,
    conv_last,
):
    n = lax.axis_size("view")
    slots = requests.shape[2]
    tiles, vox = volume.shape
    views, rows, cols = dual.shape
    wide = rows * cols
    channels = conv_second.shape[2]
    split = n in (2, 4)
    dma = pltpu.SemaphoreType.DMA
    pieces = [shape((slots, vox), BF16)] * n if split else [shape((n * slots, vox), BF16)]
    outgoing = call(
        functools.partial(gather_kernel, n, slots, split),
        pieces,
        [
            pltpu.VMEM(requests.shape, jnp.int32),
            pltpu.VMEM(counts.shape, jnp.int32),
            pltpu.VMEM(volume.shape, BF16),
            dma((3,)),
        ],
        from_hbm([requests, counts, volume]),
        [HBM] * 3,
    )
    incoming = exchange(outgoing, "view")

    small = [
        dual,
        measured,
        axial,
        conv_first.transpose(0, 1, 3, 2),
        conv_second,
        conv_last.reshape(3, 3, channels),
        slopes_first.reshape(1, channels),
        slopes_second.reshape(1, channels),
        requests,
        counts,
    ]
    flat = pltpu.VMEM((cols // LANES, views * rows, LANES), F32)
    full = (STEP + 2) * channels
    stat, foot, axial_flat, axial_back, w1, w2, w3, a1, a2, hot = call(
        functools.partial(setup_kernel, n, split),
        [
            shape((2, views, wide)),
            shape(footprint.shape, BF16),
            shape((views * rows, n * slots), BF16),
            shape((n * slots, views * rows), BF16),
            shape((BAND * channels, 144), BF16),
            shape((STEP * channels, 3 * full), BF16),
            shape((24, full), BF16),
            shape((channels, LANES)),
            shape((channels, LANES)),
            shape((tiles, n * slots), BF16),
        ],
        [
            dma((len(small) + 1,)),
            flat,
            pltpu.VMEM((views * rows, -(-n * slots // LANES) * LANES), F32),
            *[pltpu.VMEM(x.shape, x.dtype) for x in small],
        ],
        from_hbm([*small, footprint]),
        [HBM] * (len(small) + 1),
        cost=(10**8, 4 * 10**6),
    )

    message_rows = -(-9 * (wide // LANES) // 16) * 16
    edge = shape((message_rows, LANES), BF16)
    halo = pltpu.VMEM((2, message_rows, LANES), F32)
    fw, edge_a, edge_b = call(
        functools.partial(forward_kernel, n, rows),
        [shape((views, wide)), edge, edge],
        [pltpu.VMEM((n * slots, vox), BF16), flat, halo],
        [axial_flat, foot, stat, *incoming],
    )
    halo_a, halo_b = both_ways(edge_a, edge_b, "view")
    own = shape((3, views, LANES))
    strip_in, strip_msg = call(
        functools.partial(own_strip_kernel, rows), [own, own], [], [fw, stat], cost=(10**7, 10**6)
    )
    padded = 48
    strip, message = call(
        functools.partial(strip_message_kernel, rows, wide),
        [shape((3, padded, LANES)), shape((padded, LANES), BF16)],
        [pltpu.VMEM((3, padded, LANES), F32), halo],
        [strip_in, strip_msg, halo_a, halo_b],
    )
    side_a, side_b = both_ways(message, message, "col")

    def net_scratch(count, width, one=None, *lead):
        one = one or count + 4
        return [
            pltpu.VMEM((*lead, 9, -(-one // BAND) * BAND + BAND, width), F32),
            pltpu.VMEM((*lead, 3, (count + 4) * channels, width), BF16),
            pltpu.VMEM((*lead, (count + 2) * channels, width), BF16),
            pltpu.VMEM((*lead, count, width), F32),
        ]

    weights = [w1, w2, w3, a1, a2]
    ends = shape((4 * channels, wide), BF16)
    inner, one, two = call(
        inner_kernel,
        [shape((views, wide)), ends, ends],
        [pltpu.VMEM((3, views + BAND, wide), F32), *net_scratch(views - 2 * HALO, wide)],
        [fw, stat, *weights],
        cost=(2 * 10**9, 4 * 10**6),
    )
    main = call(
        outer_kernel,
        shape((views, wide)),
        [pltpu.VMEM((2, 3, 2 * BAND, wide), F32), halo, *net_scratch(HALO, wide, HALO, 2)],
        [fw, stat, halo_a, halo_b, inner, one, two, *weights],
        cost=(4 * 10**8, 2 * 10**6),
    )
    parts = [shape((slots, vox))] * n if split else [shape((n * slots, vox))]
    dual_out, *returned = call(
        functools.partial(back_kernel, n, rows),
        [shape((views * rows, cols), BF16), *parts],
        [
            pltpu.VMEM((3, padded, LANES), F32),
            *net_scratch(views, LANES),
            flat,
            pltpu.VMEM((views * rows, vox), BF16),
            pltpu.VMEM((n * slots, vox), F32),
        ],
        [strip, side_a, side_b, *weights, main, foot, axial_back],
    )
    arrived = exchange(returned, "view")
    backprojection = call(scatter_kernel, shape((tiles, vox)), [], [hot, *arrived])
    return dual_out.reshape(views, rows, cols), backprojection


def solution(mesh):
    in_specs = (
        P(("groups", "view"), "col"),
        P(("groups", "view"), None, None),
        P(("groups", "view"), None),
        P("view", None, None),
        P("view", None, "col"),
        P(("groups", "view"), None, "col"),
        P(("groups", "view"), None, "col"),
        P(),
        P(),
        P(),
        P(),
        P(),
    )
    out_specs = (P(("groups", "view"), None, "col"), P(("groups", "view"), "col"))
    return jax.shard_map(shards, mesh=mesh, in_specs=in_specs, out_specs=out_specs, check_vma=False)
```

```python
import functools

import jax
import jax.numpy as jnp
from jax import lax
from jax.experimental import pallas as pl
from jax.experimental.pallas import tpu as pltpu
from jax.sharding import PartitionSpec as P

HALO = 3
BAND = 8
STEP = 6
LANES = 128
VM = pl.BlockSpec(memory_space=pltpu.VMEM)
HBM = pl.BlockSpec(memory_space=pltpu.HBM)
F32 = jnp.float32
BF16 = jnp.bfloat16


def call(body, outs, scratch, args, specs=None, cost=None):
    single = not isinstance(outs, (list, tuple))
    return pl.pallas_call(
        body,
        out_shape=outs if single else list(outs),
        in_specs=specs or [VM] * len(args),
        out_specs=VM if single else [VM] * len(outs),
        scratch_shapes=scratch,
        compiler_params=pltpu.CompilerParams(vmem_limit_bytes=40 * 1024 * 1024),
        cost_estimate=cost and pl.CostEstimate(flops=cost[0], bytes_accessed=cost[1], transcendentals=0),
    )(*args)


def from_hbm(arrays):
    return [pltpu.with_memory_space_constraint(x, pltpu.HBM) for x in arrays]


def shape(dims, dtype=F32):
    return jax.ShapeDtypeStruct(dims, dtype)


def swap_perms(n):
    first = [(i, i ^ 1) for i in range(n)]
    second = [(i, (i + 1) % n if i % 2 else (i - 1) % n) for i in range(n)]
    return first, second


def both_ways(array_a, array_b, axis):
    first, second = swap_perms(lax.axis_size(axis))
    return lax.ppermute(array_a, axis, first), lax.ppermute(array_b, axis, second)


def order(n):
    return [0] + [k for k in (2, 3, 1) if k < n]


def partner(n, split, k):
    return lax.axis_index("view") ^ order(n)[k] if split else k


def exchange(pieces, axis):
    n = lax.axis_size(axis)
    if len(pieces) == 1:
        return [lax.all_to_all(pieces[0], axis, split_axis=0, concat_axis=0, tiled=True)]
    first, *others = pieces
    return [first] + [lax.ppermute(p, axis, [(i, i ^ k) for i in range(n)]) for p, k in zip(others, order(n)[1:])]


def iota(shape_, dim):
    return lax.broadcasted_iota(jnp.int32, shape_, dim)


def as_column(row):
    m = row.shape[1]
    spread = jnp.broadcast_to(row, (m, m))
    return jnp.sum(jnp.where(iota((m, m), 0) == iota((m, m), 1), spread, 0.0), axis=1, keepdims=True)


def wanted_row(req_ref, cnt_ref, dest):
    slots, n = req_ref.shape[2], cnt_ref.shape[1]
    row = req_ref[0, pl.ds(dest, 1), :].astype(F32)
    count = jnp.sum(jnp.where(iota((1, n), 1) == dest, cnt_ref[...].astype(F32), 0.0), axis=1, keepdims=True)
    return jnp.where(iota((1, slots), 1).astype(F32) < count, row, -1.0)


def fetch(pairs, sems):
    copies = [pltpu.make_async_copy(src, dst, sems.at[i]) for i, (src, dst) in enumerate(pairs)]
    for copy in copies:
        copy.start()
    return copies


def gather_kernel(n, slots, split, req_hbm, cnt_hbm, vol_hbm, *rest):
    outs, (req, cnt, vol, sems) = rest[:-4], rest[-4:]
    copies = fetch([(req_hbm, req), (cnt_hbm, cnt), (vol_hbm, vol)], sems)
    tiles = vol.shape[0]
    copies[0].wait()
    copies[1].wait()
    picks = []
    for k in range(n):
        column = as_column(wanted_row(req, cnt, partner(n, split, k)))
        hit = iota((slots, tiles), 1).astype(F32) == column
        picks.append(jnp.where(hit, 1.0, 0.0).astype(BF16))
    copies[2].wait()
    got = jnp.dot(jnp.concatenate(picks, axis=0), vol[...], preferred_element_type=F32).astype(BF16)
    if split:
        for k in range(n):
            outs[k][...] = got[k * slots : (k + 1) * slots, :]
    else:
        outs[0][...] = got


def scatter_kernel(hot_ref, *rest):
    pieces, out_ref = rest[:-1], rest[-1]
    left = jnp.concatenate([p[...] for p in pieces], axis=0)
    total = None
    for _ in range(3):
        part = left.astype(BF16)
        left = left - part.astype(F32)
        got = jnp.dot(hot_ref[...], part, preferred_element_type=F32)
        total = got if total is None else total + got
    out_ref[...] = total


def put_flat(flat_ref, start, block):
    for t in range(flat_ref.shape[0]):
        flat_ref[t, start : start + block.shape[0], :] = block[:, t * LANES : (t + 1) * LANES]


def widen(flat_ref, rows):
    tiles, both, _ = flat_ref.shape
    return jnp.concatenate(
        [flat_ref[t, pl.ds(r, both // rows, stride=rows), :] for r in range(rows) for t in range(tiles)], axis=1
    )


def network_weights(first, second, last, w1_ref, w2_ref, w3_ref):
    channels = second.shape[3]
    sub, view = iota((16, BAND * channels), 0), iota((16, BAND * channels), 1) // channels
    blocks = []
    for b in range(3):
        for c in range(3):
            block = jnp.zeros(sub.shape, F32)
            for a in range(3):
                row = first[a, b].astype(F32)[c : c + 1, :]
                block = jnp.where(sub == view + a, jnp.concatenate([row] * BAND, axis=1), block)
            blocks.append(block)
    depth = 16 * len(blocks)
    blocks.append(jnp.zeros((-depth % LANES, BAND * channels), F32))
    w1_ref[...] = jnp.concatenate(blocks, axis=0).T[:, 0:depth].astype(BF16)
    full = (STEP + 2) * channels
    for b in range(3):
        taps = [second[a, b].astype(F32) for a in range(3)]
        wide = jnp.concatenate(taps + [jnp.zeros((channels, full - 3 * channels), F32)], axis=1)
        for v in range(STEP):
            at = slice(v * channels, (v + 1) * channels)
            w2_ref[at, b * full : (b + 1) * full] = pltpu.roll(wide, v * channels, 1).astype(BF16)
    out = []
    sub = iota((8, full), 0)
    for b in range(3):
        taps = [last[a].astype(F32)[b : b + 1, :] for a in range(3)]
        wide = jnp.concatenate(taps + [jnp.zeros((1, full - 3 * channels), F32)], axis=1)
        wide = jnp.broadcast_to(wide, (8, full))
        block = jnp.zeros((8, full), F32)
        for v in range(STEP):
            block = jnp.where(sub == v, pltpu.roll(wide, v * channels, 1), block)
        out.append(block)
    w3_ref[...] = jnp.concatenate(out, axis=0).astype(BF16)


def setup_kernel(n, split, *refs):
    ins, outs, (sems, flat, ax_flat), local = refs[:11], refs[11:21], refs[21:24], refs[24:]
    stat_ref, foot_ref, ax_ref, back_ref, w1_ref, w2_ref, w3_ref, a1_ref, a2_ref, hot_ref = outs
    dual, meas, axial, first, second, last, slopes_1, slopes_2, req, cnt = local
    copies = fetch(list(zip(ins, (*local, foot_ref))), sems)
    for copy in copies[:-1]:
        copy.wait()
    views, rows, slots = axial.shape
    for i, ref in enumerate((dual, meas)):
        for v in range(views):
            put_flat(flat, v * rows, ref[v].astype(F32))
        stat_ref[i] = widen(flat, rows)
    ax_flat[...] = jnp.zeros(ax_flat.shape, F32)
    for v in range(views):
        ax_flat[v * rows : (v + 1) * rows, 0:slots] = axial[v].astype(F32)
    ax_ref[...] = ax_flat[:, 0:slots].astype(BF16)
    back_ref[...] = ax_flat[...].T[0:slots, :].astype(BF16)
    network_weights(first, second, last, w1_ref, w2_ref, w3_ref)
    for ref, out in ((slopes_1, a1_ref), (slopes_2, a2_ref)):
        out[...] = jnp.broadcast_to(as_column(ref[...]), out.shape)
    row = jnp.concatenate([wanted_row(req, cnt, partner(n, split, k)) for k in range(n)], axis=1)
    hit = iota(hot_ref.shape, 0).astype(F32) == row
    hot_ref[...] = jnp.where(hit, 1.0, 0.0).astype(BF16)
    copies[-1].wait()


def forward_kernel(n, rows, axial_ref, foot_ref, stat_ref, *rest):
    pieces, (fw_ref, a_ref, b_ref, slots_s, flat, edge) = rest[:-6], rest[-6:]
    me = lax.axis_index("view")
    views = foot_ref.shape[0]
    if len(pieces) > 1:
        cap = pieces[0].shape[0]
        for k in range(n):
            slots_s[pl.ds(pl.multiple_of(partner(n, True, k) * cap, cap), cap), :] = pieces[k][...]
        slot_rows = slots_s[...]
    else:
        slot_rows = pieces[0][...]
    axial_sum = jnp.dot(axial_ref[...], slot_rows, preferred_element_type=F32).astype(BF16)
    per = 16 // rows
    owner = lax.broadcasted_iota(jnp.int32, (16, foot_ref.shape[2]), 0) // rows
    for q in range(views // per):
        lhs = axial_sum[16 * q : 16 * q + 16, :]
        got = None
        for i in range(per):
            one = jnp.dot(lhs, foot_ref[q * per + i], preferred_element_type=F32)
            got = one if got is None else jnp.where(owner == i, one, got)
        put_flat(flat, 16 * q, got.astype(BF16).astype(F32))
    fw = widen(flat, rows)
    fw_ref[...] = fw
    edge[...] = jnp.zeros(edge.shape, F32)
    for way, start in ((0, 0), (1, views - HALO)):
        for c in range(3):
            part = fw[start : start + HALO, :] if c == 1 else stat_ref[c // 2, start : start + HALO, :]
            for t in range(part.shape[1] // LANES):
                at = (3 * t + c) * HALO
                edge[way, at : at + HALO, :] = part[:, t * LANES : (t + 1) * LANES]
    even = me % 2 == 0
    to_prev, to_next = edge[0], edge[1]
    a_ref[...] = jnp.where(even, to_next, to_prev).astype(BF16)
    b_ref[...] = jnp.where(even, to_prev, to_next).astype(BF16)


def sort_halo(a_ref, b_ref, halo):
    even = lax.axis_index("view") % 2 == 0
    a, b = a_ref[...].astype(F32), b_ref[...].astype(F32)
    halo[0] = jnp.where(even, b, a)
    halo[1] = jnp.where(even, a, b)


def halo_of(halo, way, channel, wide):
    starts = [(3 * t + channel) * HALO for t in range(wide // LANES)]
    return jnp.concatenate([halo[way, at : at + HALO, :] for at in starts], axis=1)


def strip_of(wide, rows, inner):
    cols = wide.shape[1] // rows
    at = iota((wide.shape[0], LANES), 1)
    total = jnp.zeros((wide.shape[0], LANES), F32)
    for r in range(rows):
        head = wide[:, r * cols : r * cols + LANES]
        tail = wide[:, (r + 1) * cols - LANES : (r + 1) * cols]
        left, right = 16 * r, 64 + 16 * r
        if inner:
            picks = ((head, 0, left + HALO, 6), (tail, LANES - 6, right, 6))
        else:
            picks = ((tail, LANES - HALO, left, HALO), (head, 0, right + 6, HALO))
        for source, begin, target, width in picks:
            moved = pltpu.roll(source, (target - begin) % LANES, 1)
            total = jnp.where((at >= target) & (at < target + width), moved, total)
    return total


def own_strip_kernel(rows, fw_ref, stat_ref, in_ref, msg_ref):
    for c in range(3):
        wide = fw_ref[...] if c == 1 else stat_ref[c // 2]
        in_ref[c] = strip_of(wide, rows, True)
        msg_ref[c] = strip_of(wide, rows, False)


def strip_message_kernel(rows, wide, in_ref, msg_ref, a_ref, b_ref, strip_ref, out_ref, buf, halo):
    views = in_ref.shape[1]
    sort_halo(a_ref, b_ref, halo)
    buf[...] = jnp.zeros(buf.shape, F32)
    strip_ref[...] = jnp.zeros(strip_ref.shape, F32)
    for c in range(3):
        for way, start in ((0, 0), (1, HALO + views)):
            part = halo_of(halo, way, c, wide)
            strip_ref[c, start : start + HALO, :] = strip_of(part, rows, True)
            buf[c, start : start + HALO, :] = strip_of(part, rows, False)
        strip_ref[c, HALO : HALO + views, :] = in_ref[c]
        buf[c, HALO : HALO + views, :] = msg_ref[c]
    total = buf[0] + pltpu.roll(buf[1], HALO, 1) + pltpu.roll(buf[2], 2 * HALO, 1)
    out_ref[...] = total.astype(BF16)


def prelu(z, slopes_ref):
    channels = slopes_ref.shape[0]
    slopes = jnp.concatenate([slopes_ref[...]] * (z.shape[0] // channels), axis=0)
    slopes = jnp.concatenate([slopes] * (z.shape[1] // LANES), axis=1)
    return jnp.maximum(z, slopes * z)


def shifted(z):
    return pltpu.roll(z, 1, 1), z, pltpu.roll(z, z.shape[1] - 1, 1)


def chunks(ref):
    n = ref.shape[-1]
    width = min(n, 2 * LANES)
    return [slice(i, i + width) for i in range(0, n, width)]


def first_layer(inputs, count, w1, a1, s1, s2, base=0, inside=None):
    channels = a1.shape[0]
    for at in chunks(s2):
        for c in range(3):
            for b, x in enumerate(shifted(inputs(c, at))):
                s1[3 * b + c, :, at] = x
    for k in range(-(-count // BAND)):
        for at in chunks(s2):
            m = min(BAND, count - BAND * k) * channels
            window = jnp.concatenate([s1[j, BAND * k : BAND * k + 16, at] for j in range(9)], axis=0).astype(BF16)
            z = prelu(jnp.dot(w1[0:m, :], window, preferred_element_type=F32), a1)
            if inside is not None:
                z = jnp.where(inside, z, 0.0)
            row = base + BAND * k * channels
            for b, x in enumerate(shifted(z.astype(BF16))):
                s2[b, row : row + m, at] = x


def second_layer(count, w2, a2, s2, s3, base=0, inside=None):
    channels = a2.shape[0]
    full = (STEP + 2) * channels
    for k in range(-(-count // STEP)):
        part = min(STEP, count - STEP * k)
        m, depth = part * channels, (part + 2) * channels
        begin = STEP * k * channels
        for at in chunks(s2):
            windows = [s2[b, begin : begin + depth, at] for b in range(3)]
            if part == STEP:
                z = jnp.dot(w2[...], jnp.concatenate(windows, axis=0), preferred_element_type=F32)
            else:
                z = sum(
                    jnp.dot(w2[0:m, b * full : b * full + depth], windows[b], preferred_element_type=F32) for b in range(3)
                )
            z = prelu(z, a2)
            if inside is not None:
                z = jnp.where(inside, z, 0.0)
            s3[base + begin : base + begin + m, at] = z.astype(BF16)


def last_layer(count, channels, w3, s3, update):
    for k in range(-(-count // STEP)):
        part = min(STEP, count - STEP * k)
        begin, depth = STEP * k * channels, (part + 2) * channels
        for at in chunks(s3):
            got = jnp.dot(w3[:, 0:depth], s3[begin : begin + depth, at], preferred_element_type=F32)
            n = got.shape[1]
            out = pltpu.roll(got[0:8], 1, 1) + got[8:16] + pltpu.roll(got[16:24], n - 1, 1)
            update[STEP * k : STEP * k + part, at] = out[0:part, :]


def inner_kernel(fw_ref, stat_ref, w1, w2, w3, a1, a2, out_ref, one_ref, two_ref, x, s1, s2, s3, update):
    views = fw_ref.shape[0]
    channels = a1.shape[0]
    x[...] = jnp.zeros(x.shape, F32)
    for c in range(3):
        x[c, 0:views, :] = fw_ref[...] if c == 1 else stat_ref[c // 2]
    first_layer(lambda c, at: x[c, :, at], views - 2, w1, a1, s1, s2)
    second_layer(views - 4, w2, a2, s2, s3)
    last_layer(views - 6, channels, w3, s3, update)
    out_ref[HALO : views - HALO, :] = stat_ref[0, HALO : views - HALO, :] + update[...]
    two = 2 * channels
    for ref, ends in ((one_ref, s2.at[1]), (two_ref, s3)):
        end = ends.shape[0]
        ref[0:two, :] = ends[0:two, :]
        ref[two : 2 * two, :] = ends[end - two : end, :]


def outer_kernel(
    fw_ref, stat_ref, ha_ref, hb_ref, in_ref, one_ref, two_ref, w1, w2, w3, a1, a2, out_ref, x, halo, s1, s2, s3, update
):
    views, wide = fw_ref.shape
    channels = a1.shape[0]
    sort_halo(ha_ref, hb_ref, halo)
    x[...] = jnp.zeros(x.shape, F32)
    for c in range(3):
        x[0, c, 0:HALO, :] = halo_of(halo, 0, c, wide)
        x[1, c, 2 : 2 + HALO, :] = halo_of(halo, 1, c, wide)
        source = fw_ref if c == 1 else stat_ref.at[c // 2]
        x[0, c, HALO : HALO + 2, :] = source[0:2, :]
        x[1, c, 0:2, :] = source[views - 2 : views, :]
    two = 2 * channels
    new, old = (0, two), (HALO * channels, 0)
    for side in range(2):
        kept = slice(side * two, (side + 1) * two)
        for at in chunks(one_ref):
            for b, moved in enumerate(shifted(one_ref[kept, at])):
                s2[side, b, old[side] : old[side] + two, at] = moved
        s3[side, old[side] : old[side] + two, :] = two_ref[kept, :]
    for side in range(2):
        first_layer(lambda c, at: x[side, c, :, at], HALO, w1, a1, s1.at[side], s2.at[side], new[side])
    for side in range(2):
        second_layer(HALO, w2, a2, s2.at[side], s3.at[side], new[side])
    for side in range(2):
        last_layer(HALO, channels, w3, s3.at[side], update.at[side])
    out_ref[HALO : views - HALO, :] = in_ref[HALO : views - HALO, :]
    for side, begin in ((0, 0), (1, views - HALO)):
        out_ref[begin : begin + HALO, :] = stat_ref[0, begin : begin + HALO, :] + update[side]


def back_kernel(
    n, rows, strip_ref, ra_ref, rb_ref, w1, w2, w3, a1, a2, main_ref, foot_ref, axial_ref, dual_ref, *rest
):
    parts, (x, s1, s2, s3, update, flat, back, part_s) = rest[:-8], rest[-8:]
    views, _, cols = foot_ref.shape[0], foot_ref.shape[1], foot_ref.shape[2]
    me, peers = lax.axis_index("col"), lax.axis_size("col")
    even = me % 2 == 0
    at = iota((1, LANES), 1)
    left_side, step = at < 64, at % 16
    from_left = left_side & (step < HALO) & (me > 0)
    from_right = (~left_side) & (step >= 6) & (step < 9) & (me < peers - 1)
    inside = (left_side & ((step >= HALO) | (me > 0))) | ((~left_side) & ((step < 6) | (me < peers - 1)))
    a, b = ra_ref[...].astype(F32), rb_ref[...].astype(F32)
    sides = jnp.where(at < 64, jnp.where(even, b, a), jnp.where(even, a, b))
    half = views // 2
    for c in range(3):
        side = pltpu.roll(sides, (-HALO * c) % LANES, 1)
        joined = jnp.where(from_left | from_right, side, strip_ref[c])
        x[c, :, 0:LANES] = joined[0 : x.shape[1], :]
        x[c, :, LANES:] = joined[half : half + x.shape[1], :]
    inside = jnp.concatenate([inside, inside], axis=1)
    first_layer(lambda c, at: x[c, :, at], half + 4, w1, a1, s1, s2, 0, inside)
    second_layer(half + 2, w2, a2, s2, s3, 0, inside)
    last_layer(half, a1.shape[0], w3, s3, update)
    strip = x[0, HALO : HALO + half, :] + update[...]
    strip = jnp.concatenate([strip[:, 0:LANES], strip[:, LANES:]], axis=0)
    first = iota((views, LANES), 1)
    for r in range(rows):
        head = main_ref[:, r * cols : r * cols + LANES]
        tail = main_ref[:, (r + 1) * cols - LANES : (r + 1) * cols]
        moved = pltpu.roll(strip, (-(16 * r + HALO)) % LANES, 1)
        head = jnp.where(first < HALO, moved, head)
        moved = pltpu.roll(strip, (LANES - HALO - (64 + 16 * r + HALO)) % LANES, 1)
        tail = jnp.where(first >= LANES - HALO, moved, tail)
        for t in range(cols // LANES):
            middle = main_ref[:, r * cols + t * LANES : r * cols + (t + 1) * LANES]
            last = cols // LANES - 1
            flat[t, pl.ds(r, views, stride=rows), :] = head if t == 0 else tail if t == last else middle
    per = 16 // rows
    owner = lax.broadcasted_iota(jnp.int32, (16, foot_ref.shape[1]), 0) // rows
    for q in range(views // per):
        block = jnp.concatenate([flat[t, 16 * q : 16 * q + 16, :] for t in range(cols // LANES)], axis=1).astype(BF16)
        dual_ref[16 * q : 16 * q + 16, :] = block
        got = None
        for i in range(per):
            one = lax.dot_general(
                block, foot_ref[q * per + i], (((1,), (1,)), ((), ())), preferred_element_type=F32
            )
            got = one if got is None else jnp.where(owner == i, one, got)
        back[16 * q : 16 * q + 16, :] = got.astype(BF16)
    partial = jnp.dot(axial_ref[...], back[...], preferred_element_type=F32)
    if len(parts) > 1:
        part_s[...] = partial
        cap = parts[0].shape[0]
        for k in range(n):
            parts[k][...] = part_s[pl.ds(pl.multiple_of(partner(n, True, k) * cap, cap), cap), :]
    else:
        parts[0][...] = partial


def shards(
    volume,
    requests,
    counts,
    axial,
    footprint,
    dual,
    measured,
    conv_first,
    slopes_first,
    conv_second,
    slopes_second,
    conv_last,
):
    n = lax.axis_size("view")
    slots = requests.shape[2]
    tiles, vox = volume.shape
    views, rows, cols = dual.shape
    wide = rows * cols
    channels = conv_second.shape[2]
    split = n in (2, 4)
    dma = pltpu.SemaphoreType.DMA
    pieces = [shape((slots, vox), BF16)] * n if split else [shape((n * slots, vox), BF16)]
    outgoing = call(
        functools.partial(gather_kernel, n, slots, split),
        pieces,
        [
            pltpu.VMEM(requests.shape, jnp.int32),
            pltpu.VMEM(counts.shape, jnp.int32),
            pltpu.VMEM(volume.shape, BF16),
            dma((3,)),
        ],
        from_hbm([requests, counts, volume]),
        [HBM] * 3,
    )
    incoming = exchange(outgoing, "view")

    small = [
        dual,
        measured,
        axial,
        conv_first.transpose(0, 1, 3, 2),
        conv_second,
        conv_last.reshape(3, 3, channels),
        slopes_first.reshape(1, channels),
        slopes_second.reshape(1, channels),
        requests,
        counts,
    ]
    flat = pltpu.VMEM((cols // LANES, views * rows, LANES), F32)
    full = (STEP + 2) * channels
    stat, foot, axial_flat, axial_back, w1, w2, w3, a1, a2, hot = call(
        functools.partial(setup_kernel, n, split),
        [
            shape((2, views, wide)),
            shape(footprint.shape, BF16),
            shape((views * rows, n * slots), BF16),
            shape((n * slots, views * rows), BF16),
            shape((BAND * channels, 144), BF16),
            shape((STEP * channels, 3 * full), BF16),
            shape((24, full), BF16),
            shape((channels, LANES)),
            shape((channels, LANES)),
            shape((tiles, n * slots), BF16),
        ],
        [
            dma((len(small) + 1,)),
            flat,
            pltpu.VMEM((views * rows, -(-n * slots // LANES) * LANES), F32),
            *[pltpu.VMEM(x.shape, x.dtype) for x in small],
        ],
        from_hbm([*small, footprint]),
        [HBM] * (len(small) + 1),
        cost=(10**8, 4 * 10**6),
    )

    message_rows = -(-9 * (wide // LANES) // 16) * 16
    edge = shape((message_rows, LANES), BF16)
    halo = pltpu.VMEM((2, message_rows, LANES), F32)
    fw, edge_a, edge_b = call(
        functools.partial(forward_kernel, n, rows),
        [shape((views, wide)), edge, edge],
        [pltpu.VMEM((n * slots, vox), BF16), flat, halo],
        [axial_flat, foot, stat, *incoming],
    )
    halo_a, halo_b = both_ways(edge_a, edge_b, "view")
    own = shape((3, views, LANES))
    strip_in, strip_msg = call(
        functools.partial(own_strip_kernel, rows), [own, own], [], [fw, stat], cost=(10**7, 10**6)
    )
    padded = 48
    strip, message = call(
        functools.partial(strip_message_kernel, rows, wide),
        [shape((3, padded, LANES)), shape((padded, LANES), BF16)],
        [pltpu.VMEM((3, padded, LANES), F32), halo],
        [strip_in, strip_msg, halo_a, halo_b],
    )
    side_a, side_b = both_ways(message, message, "col")

    def net_scratch(count, width, one=None, *lead):
        one = one or count + 4
        return [
            pltpu.VMEM((*lead, 9, -(-one // BAND) * BAND + BAND, width), F32),
            pltpu.VMEM((*lead, 3, (count + 4) * channels, width), BF16),
            pltpu.VMEM((*lead, (count + 2) * channels, width), BF16),
            pltpu.VMEM((*lead, count, width), F32),
        ]

    weights = [w1, w2, w3, a1, a2]
    ends = shape((4 * channels, wide), BF16)
    inner, one, two = call(
        inner_kernel,
        [shape((views, wide)), ends, ends],
        [pltpu.VMEM((3, views + BAND, wide), F32), *net_scratch(views - 2 * HALO, wide)],
        [fw, stat, *weights],
        cost=(2 * 10**9, 4 * 10**6),
    )
    main = call(
        outer_kernel,
        shape((views, wide)),
        [pltpu.VMEM((2, 3, 2 * BAND, wide), F32), halo, *net_scratch(HALO, wide, HALO, 2)],
        [fw, stat, halo_a, halo_b, inner, one, two, *weights],
        cost=(4 * 10**8, 2 * 10**6),
    )
    parts = [shape((slots, vox))] * n if split else [shape((n * slots, vox))]
    dual_out, *returned = call(
        functools.partial(back_kernel, n, rows),
        [shape((views * rows, cols), BF16), *parts],
        [
            pltpu.VMEM((3, padded - views // 2, 2 * LANES), F32),
            *net_scratch(views // 2, 2 * LANES),
            flat,
            pltpu.VMEM((views * rows, vox), BF16),
            pltpu.VMEM((n * slots, vox), F32),
        ],
        [strip, side_a, side_b, *weights, main, foot, axial_back],
    )
    arrived = exchange(returned, "view")
    backprojection = call(scatter_kernel, shape((tiles, vox)), [], [hot, *arrived])
    return dual_out.reshape(views, rows, cols), backprojection


def solution(mesh):
    in_specs = (
        P(("groups", "view"), "col"),
        P(("groups", "view"), None, None),
        P(("groups", "view"), None),
        P("view", None, None),
        P("view", None, "col"),
        P(("groups", "view"), None, "col"),
        P(("groups", "view"), None, "col"),
        P(),
        P(),
        P(),
        P(),
        P(),
    )
    out_specs = (P(("groups", "view"), None, "col"), P(("groups", "view"), "col"))
    return jax.shard_map(shards, mesh=mesh, in_specs=in_specs, out_specs=out_specs, check_vma=False)
```

```python
import functools

import jax
import jax.numpy as jnp
from jax import lax
from jax.experimental import pallas as pl
from jax.experimental.pallas import tpu as pltpu
from jax.sharding import PartitionSpec as P

HALO = 3
BAND = 8
STEP = 6
LANES = 128
VM = pl.BlockSpec(memory_space=pltpu.VMEM)
HBM = pl.BlockSpec(memory_space=pltpu.HBM)
F32 = jnp.float32
BF16 = jnp.bfloat16


def call(body, outs, scratch, args, specs=None, cost=None):
    single = not isinstance(outs, (list, tuple))
    return pl.pallas_call(
        body,
        out_shape=outs if single else list(outs),
        in_specs=specs or [VM] * len(args),
        out_specs=VM if single else [VM] * len(outs),
        scratch_shapes=scratch,
        compiler_params=pltpu.CompilerParams(vmem_limit_bytes=40 * 1024 * 1024),
        cost_estimate=cost and pl.CostEstimate(flops=cost[0], bytes_accessed=cost[1], transcendentals=0),
    )(*args)


def from_hbm(arrays):
    return [pltpu.with_memory_space_constraint(x, pltpu.HBM) for x in arrays]


def shape(dims, dtype=F32):
    return jax.ShapeDtypeStruct(dims, dtype)


def swap_perms(n):
    first = [(i, i ^ 1) for i in range(n)]
    second = [(i, (i + 1) % n if i % 2 else (i - 1) % n) for i in range(n)]
    return first, second


def both_ways(array_a, array_b, axis):
    first, second = swap_perms(lax.axis_size(axis))
    return lax.ppermute(array_a, axis, first), lax.ppermute(array_b, axis, second)


def order(n):
    return [0] + [k for k in (2, 3, 1) if k < n]


def partner(n, split, k):
    return lax.axis_index("view") ^ order(n)[k] if split else k


def exchange(pieces, axis):
    n = lax.axis_size(axis)
    if len(pieces) == 1:
        return [lax.all_to_all(pieces[0], axis, split_axis=0, concat_axis=0, tiled=True)]
    first, *others = pieces
    return [first] + [lax.ppermute(p, axis, [(i, i ^ k) for i in range(n)]) for p, k in zip(others, order(n)[1:])]


def iota(shape_, dim):
    return lax.broadcasted_iota(jnp.int32, shape_, dim)


def as_column(row):
    m = row.shape[1]
    spread = jnp.broadcast_to(row, (m, m))
    return jnp.sum(jnp.where(iota((m, m), 0) == iota((m, m), 1), spread, 0.0), axis=1, keepdims=True)


def wanted_row(req_ref, cnt_ref, dest):
    slots, n = req_ref.shape[2], cnt_ref.shape[1]
    row = req_ref[0, pl.ds(dest, 1), :].astype(F32)
    count = jnp.sum(jnp.where(iota((1, n), 1) == dest, cnt_ref[...].astype(F32), 0.0), axis=1, keepdims=True)
    return jnp.where(iota((1, slots), 1).astype(F32) < count, row, -1.0)


def fetch(pairs, sems):
    copies = [pltpu.make_async_copy(src, dst, sems.at[i]) for i, (src, dst) in enumerate(pairs)]
    for copy in copies:
        copy.start()
    return copies


def gather_kernel(n, slots, split, req_hbm, cnt_hbm, vol_hbm, *rest):
    outs, (req, cnt, vol, sems) = rest[:-4], rest[-4:]
    copies = fetch([(req_hbm, req), (cnt_hbm, cnt), (vol_hbm, vol)], sems)
    tiles = vol.shape[0]
    copies[0].wait()
    copies[1].wait()
    picks = []
    for k in range(n):
        column = as_column(wanted_row(req, cnt, partner(n, split, k)))
        hit = iota((slots, tiles), 1).astype(F32) == column
        picks.append(jnp.where(hit, 1.0, 0.0).astype(BF16))
    copies[2].wait()
    got = jnp.dot(jnp.concatenate(picks, axis=0), vol[...], preferred_element_type=F32).astype(BF16)
    if split:
        for k in range(n):
            outs[k][...] = got[k * slots : (k + 1) * slots, :]
    else:
        outs[0][...] = got


def scatter_kernel(hot_ref, *rest):
    pieces, out_ref = rest[:-1], rest[-1]
    left = jnp.concatenate([p[...] for p in pieces], axis=0)
    total = None
    for _ in range(3):
        part = left.astype(BF16)
        left = left - part.astype(F32)
        got = jnp.dot(hot_ref[...], part, preferred_element_type=F32)
        total = got if total is None else total + got
    out_ref[...] = total


def put_flat(flat_ref, start, block):
    for t in range(flat_ref.shape[0]):
        flat_ref[t, start : start + block.shape[0], :] = block[:, t * LANES : (t + 1) * LANES]


def widen(flat_ref, rows):
    tiles, both, _ = flat_ref.shape
    return jnp.concatenate(
        [flat_ref[t, pl.ds(r, both // rows, stride=rows), :] for r in range(rows) for t in range(tiles)], axis=1
    )


def network_weights(first, second, last, w1_ref, w2_ref, w3_ref):
    channels = second.shape[3]
    sub, view = iota((16, BAND * channels), 0), iota((16, BAND * channels), 1) // channels
    blocks = []
    for b in range(3):
        for c in range(3):
            block = jnp.zeros(sub.shape, F32)
            for a in range(3):
                row = first[a, b].astype(F32)[c : c + 1, :]
                block = jnp.where(sub == view + a, jnp.concatenate([row] * BAND, axis=1), block)
            blocks.append(block)
    depth = 16 * len(blocks)
    blocks.append(jnp.zeros((-depth % LANES, BAND * channels), F32))
    w1_ref[...] = jnp.concatenate(blocks, axis=0).T[:, 0:depth].astype(BF16)
    full = (STEP + 2) * channels
    for b in range(3):
        taps = [second[a, b].astype(F32) for a in range(3)]
        wide = jnp.concatenate(taps + [jnp.zeros((channels, full - 3 * channels), F32)], axis=1)
        for v in range(STEP):
            at = slice(v * channels, (v + 1) * channels)
            w2_ref[at, b * full : (b + 1) * full] = pltpu.roll(wide, v * channels, 1).astype(BF16)
    out = []
    sub = iota((8, full), 0)
    for b in range(3):
        taps = [last[a].astype(F32)[b : b + 1, :] for a in range(3)]
        wide = jnp.concatenate(taps + [jnp.zeros((1, full - 3 * channels), F32)], axis=1)
        wide = jnp.broadcast_to(wide, (8, full))
        block = jnp.zeros((8, full), F32)
        for v in range(STEP):
            block = jnp.where(sub == v, pltpu.roll(wide, v * channels, 1), block)
        out.append(block)
    w3_ref[...] = jnp.concatenate(out, axis=0).astype(BF16)


def setup_kernel(n, split, *refs):
    ins, outs, (sems, flat, ax_flat), local = refs[:11], refs[11:21], refs[21:24], refs[24:]
    stat_ref, foot_ref, ax_ref, back_ref, w1_ref, w2_ref, w3_ref, a1_ref, a2_ref, hot_ref = outs
    dual, meas, axial, first, second, last, slopes_1, slopes_2, req, cnt = local
    copies = fetch(list(zip(ins, (*local, foot_ref))), sems)
    for copy in copies[:-1]:
        copy.wait()
    views, rows, slots = axial.shape
    for i, ref in enumerate((dual, meas)):
        for v in range(views):
            put_flat(flat, v * rows, ref[v].astype(F32))
        stat_ref[i] = widen(flat, rows)
    ax_flat[...] = jnp.zeros(ax_flat.shape, F32)
    for v in range(views):
        ax_flat[v * rows : (v + 1) * rows, 0:slots] = axial[v].astype(F32)
    ax_ref[...] = ax_flat[:, 0:slots].astype(BF16)
    back_ref[...] = ax_flat[...].T[0:slots, :].astype(BF16)
    network_weights(first, second, last, w1_ref, w2_ref, w3_ref)
    for ref, out in ((slopes_1, a1_ref), (slopes_2, a2_ref)):
        out[...] = jnp.broadcast_to(as_column(ref[...]), out.shape)
    row = jnp.concatenate([wanted_row(req, cnt, partner(n, split, k)) for k in range(n)], axis=1)
    hit = iota(hot_ref.shape, 0).astype(F32) == row
    hot_ref[...] = jnp.where(hit, 1.0, 0.0).astype(BF16)
    copies[-1].wait()


def project(lhs, foot_ref, start, rows):
    owner = iota((16, foot_ref.shape[2]), 0) // rows
    got = None
    for i in range(16 // rows):
        one = jnp.dot(lhs, foot_ref[start + i], preferred_element_type=F32)
        got = one if got is None else jnp.where(owner == i, one, got)
    return got.astype(BF16).astype(F32)


def edge_kernel(n, rows, axial_ref, foot_ref, stat_ref, *rest):
    pieces, (slots_ref, a_ref, b_ref, flat, edge) = rest[:-5], rest[-5:]
    views = foot_ref.shape[0]
    if len(pieces) > 1:
        cap = pieces[0].shape[0]
        for k in range(n):
            slots_ref[pl.ds(pl.multiple_of(partner(n, True, k) * cap, cap), cap), :] = pieces[k][...]
    else:
        slots_ref[...] = pieces[0][...]
    per, both = 16 // rows, views * rows
    ends = jnp.concatenate([axial_ref[0:16, :], axial_ref[both - 16 : both, :]], axis=0)
    axial_sum = jnp.dot(ends, slots_ref[...], preferred_element_type=F32).astype(BF16)
    for way, start in ((0, 0), (1, views - per)):
        put_flat(flat, 16 * way, project(axial_sum[16 * way : 16 * way + 16, :], foot_ref, start, rows))
    edge[...] = jnp.zeros(edge.shape, F32)
    tiles = flat.shape[0]
    for way, start in ((0, 0), (1, views - HALO)):
        first = 16 * way + (start - way * (views - per)) * rows
        for r in range(rows):
            for t in range(tiles):
                at = 3 * (r * tiles + t) * HALO
                lanes = slice((r * tiles + t) * LANES, (r * tiles + t + 1) * LANES)
                edge[way, at : at + HALO, :] = stat_ref[0, start : start + HALO, lanes]
                edge[way, at + HALO : at + 2 * HALO, :] = flat[t, pl.ds(first + r, HALO, stride=rows), :]
                edge[way, at + 2 * HALO : at + 3 * HALO, :] = stat_ref[1, start : start + HALO, lanes]
    even = lax.axis_index("view") % 2 == 0
    to_prev, to_next = edge[0], edge[1]
    a_ref[...] = jnp.where(even, to_next, to_prev).astype(BF16)
    b_ref[...] = jnp.where(even, to_prev, to_next).astype(BF16)


def forward_kernel(rows, axial_ref, foot_ref, slots_ref, ends_ref, fw_ref, flat):
    axial_sum = jnp.dot(axial_ref[...], slots_ref[...], preferred_element_type=F32).astype(BF16)
    per, both = 16 // rows, flat.shape[1]
    for q in range(1, both // 16 - 1):
        put_flat(flat, 16 * q, project(axial_sum[16 * q : 16 * q + 16, :], foot_ref, q * per, rows))
    flat[:, 0:16, :] = ends_ref[:, 0:16, :]
    flat[:, both - 16 : both, :] = ends_ref[:, 16:32, :]
    fw_ref[...] = widen(flat, rows)


def sort_halo(a_ref, b_ref, halo):
    even = lax.axis_index("view") % 2 == 0
    a, b = a_ref[...].astype(F32), b_ref[...].astype(F32)
    halo[0] = jnp.where(even, b, a)
    halo[1] = jnp.where(even, a, b)


def halo_of(halo, way, channel, wide):
    starts = [(3 * t + channel) * HALO for t in range(wide // LANES)]
    return jnp.concatenate([halo[way, at : at + HALO, :] for at in starts], axis=1)


def strip_of(tile, rows, tiles, inner):
    total = None
    for r in range(rows):
        head, tail = tile(r * tiles), tile((r + 1) * tiles - 1)
        at = iota(head.shape, 1)
        left, right = 16 * r, 64 + 16 * r
        if inner:
            picks = ((head, 0, left + HALO, 6), (tail, LANES - 6, right, 6))
        else:
            picks = ((tail, LANES - HALO, left, HALO), (head, 0, right + 6, HALO))
        for source, begin, target, width in picks:
            moved = pltpu.roll(source, (target - begin) % LANES, 1)
            rest = jnp.zeros_like(moved) if total is None else total
            total = jnp.where((at >= target) & (at < target + width), moved, rest)
    return total


def joined(parts):
    return parts[0] + pltpu.roll(parts[1], HALO, 1) + pltpu.roll(parts[2], 2 * HALO, 1)


def own_strips(rows, fw_ref, stat_ref, inner):
    tiles = fw_ref.shape[1] // rows // LANES
    sources = (stat_ref.at[0], fw_ref, stat_ref.at[1])
    get = [lambda i, ref=ref: ref[:, i * LANES : (i + 1) * LANES] for ref in sources]
    return [strip_of(tile, rows, tiles, inner) for tile in get]


def own_message_kernel(rows, fw_ref, stat_ref, msg_ref):
    msg_ref[...] = joined(own_strips(rows, fw_ref, stat_ref, False))


def halo_strip(halo, way, rows, tiles, inner):
    return strip_of(lambda i: halo[way, 3 * i * HALO : 3 * (i + 1) * HALO, :], rows, tiles, inner)


def strip_message_kernel(rows, tiles, msg_ref, a_ref, b_ref, out_ref, buf, halo):
    views = msg_ref.shape[0]
    sort_halo(a_ref, b_ref, halo)
    buf[HALO + views :, :] = jnp.zeros((buf.shape[0] - HALO - views, LANES), F32)
    buf[HALO : HALO + views, :] = msg_ref[...]
    for way, start in ((0, 0), (1, HALO + views)):
        part = halo_strip(halo, way, rows, tiles, False)
        buf[start : start + HALO, :] = joined([part[c * HALO : (c + 1) * HALO, :] for c in range(3)])
    out_ref[...] = buf[...].astype(BF16)


def prelu(z, slopes_ref):
    channels = slopes_ref.shape[0]
    slopes = jnp.concatenate([slopes_ref[...]] * (z.shape[0] // channels), axis=0)
    slopes = jnp.concatenate([slopes] * (z.shape[1] // LANES), axis=1)
    return jnp.maximum(z, slopes * z)


def shifted(z):
    return pltpu.roll(z, 1, 1), z, pltpu.roll(z, z.shape[1] - 1, 1)


def chunks(ref):
    n = ref.shape[-1]
    width = min(n, 2 * LANES)
    return [slice(i, i + width) for i in range(0, n, width)]


def first_layer(inputs, count, w1, a1, s1, s2, base=0, inside=None):
    channels = a1.shape[0]
    for at in chunks(s2):
        for c in range(3):
            for b, x in enumerate(shifted(inputs(c, at))):
                s1[3 * b + c, :, at] = x
    for k in range(-(-count // BAND)):
        for at in chunks(s2):
            m = min(BAND, count - BAND * k) * channels
            window = jnp.concatenate([s1[j, BAND * k : BAND * k + 16, at] for j in range(9)], axis=0).astype(BF16)
            z = prelu(jnp.dot(w1[0:m, :], window, preferred_element_type=F32), a1)
            if inside is not None:
                z = jnp.where(inside, z, 0.0)
            row = base + BAND * k * channels
            for b, x in enumerate(shifted(z.astype(BF16))):
                s2[b, row : row + m, at] = x


def second_layer(count, w2, a2, s2, s3, base=0, inside=None):
    channels = a2.shape[0]
    full = (STEP + 2) * channels
    for k in range(-(-count // STEP)):
        part = min(STEP, count - STEP * k)
        m, depth = part * channels, (part + 2) * channels
        begin = STEP * k * channels
        for at in chunks(s2):
            windows = [s2[b, begin : begin + depth, at] for b in range(3)]
            if part == STEP:
                z = jnp.dot(w2[...], jnp.concatenate(windows, axis=0), preferred_element_type=F32)
            else:
                z = sum(
                    jnp.dot(w2[0:m, b * full : b * full + depth], windows[b], preferred_element_type=F32) for b in range(3)
                )
            z = prelu(z, a2)
            if inside is not None:
                z = jnp.where(inside, z, 0.0)
            s3[base + begin : base + begin + m, at] = z.astype(BF16)


def last_layer(count, channels, w3, s3, update):
    for k in range(-(-count // STEP)):
        part = min(STEP, count - STEP * k)
        begin, depth = STEP * k * channels, (part + 2) * channels
        for at in chunks(s3):
            got = jnp.dot(w3[:, 0:depth], s3[begin : begin + depth, at], preferred_element_type=F32)
            n = got.shape[1]
            out = pltpu.roll(got[0:8], 1, 1) + got[8:16] + pltpu.roll(got[16:24], n - 1, 1)
            update[STEP * k : STEP * k + part, at] = out[0:part, :]


def inner_kernel(fw_ref, stat_ref, w1, w2, a1, a2, one_ref, s3, x, s1, s2):
    views = fw_ref.shape[0]
    x[...] = jnp.zeros(x.shape, F32)
    for c in range(3):
        x[c, 0:views, :] = fw_ref[...] if c == 1 else stat_ref[c // 2]
    first_layer(lambda c, at: x[c, :, at], views - 2, w1, a1, s1, s2)
    second_layer(views - 4, w2, a2, s2, s3)
    two, end = 2 * a1.shape[0], s2.shape[1]
    one_ref[0:two, :] = s2[1, 0:two, :]
    one_ref[two : 2 * two, :] = s2[1, end - two : end, :]


def outer_kernel(
    rows, fw_ref, stat_ref, ha_ref, hb_ref, one_ref, two_ref, w1, w2, w3, a1, a2, out_ref, strip_ref, x, halo, s1, s2, s3,
    update, inner
):
    views, wide = fw_ref.shape
    channels = a1.shape[0]
    sort_halo(ha_ref, hb_ref, halo)
    strip_ref[...] = jnp.zeros(strip_ref.shape, F32)
    for way, start in ((0, 0), (1, HALO + views)):
        part = halo_strip(halo, way, rows, wide // rows // LANES, True)
        for c in range(3):
            strip_ref[c, start : start + HALO, :] = part[c * HALO : (c + 1) * HALO, :]
    for c, own in enumerate(own_strips(rows, fw_ref, stat_ref, True)):
        strip_ref[c, HALO : HALO + views, :] = own
    x[...] = jnp.zeros(x.shape, F32)
    for c in range(3):
        x[0, c, 0:HALO, :] = halo_of(halo, 0, c, wide)
        x[1, c, 2 : 2 + HALO, :] = halo_of(halo, 1, c, wide)
        source = fw_ref if c == 1 else stat_ref.at[c // 2]
        x[0, c, HALO : HALO + 2, :] = source[0:2, :]
        x[1, c, 0:2, :] = source[views - 2 : views, :]
    two = 2 * channels
    new, old = (0, two), (HALO * channels, 0)
    for side in range(2):
        kept = slice(side * two, (side + 1) * two)
        for at in chunks(one_ref):
            for b, moved in enumerate(shifted(one_ref[kept, at])):
                s2[side, b, old[side] : old[side] + two, at] = moved
        end = side * (two_ref.shape[0] - two)
        s3[side, old[side] : old[side] + two, :] = two_ref[end : end + two, :]
    for side in range(2):
        first_layer(lambda c, at: x[side, c, :, at], HALO, w1, a1, s1.at[side], s2.at[side], new[side])
    for side in range(2):
        second_layer(HALO, w2, a2, s2.at[side], s3.at[side], new[side])
    for side in range(2):
        last_layer(HALO, channels, w3, s3.at[side], update.at[side])
    last_layer(views - 2 * HALO, channels, w3, two_ref, inner)
    out_ref[HALO : views - HALO, :] = stat_ref[0, HALO : views - HALO, :] + inner[...]
    for side, begin in ((0, 0), (1, views - HALO)):
        out_ref[begin : begin + HALO, :] = stat_ref[0, begin : begin + HALO, :] + update[side]


def back_kernel(
    n, rows, strip_ref, ra_ref, rb_ref, w1, w2, w3, a1, a2, main_ref, foot_ref, axial_ref, dual_ref, *rest
):
    parts, (x, s1, s2, s3, update, flat, back, part_s) = rest[:-8], rest[-8:]
    views, _, cols = foot_ref.shape[0], foot_ref.shape[1], foot_ref.shape[2]
    me, peers = lax.axis_index("col"), lax.axis_size("col")
    even = me % 2 == 0
    at = iota((1, LANES), 1)
    left_side, step = at < 64, at % 16
    from_left = left_side & (step < HALO) & (me > 0)
    from_right = (~left_side) & (step >= 6) & (step < 9) & (me < peers - 1)
    inside = (left_side & ((step >= HALO) | (me > 0))) | ((~left_side) & ((step < 6) | (me < peers - 1)))
    a, b = ra_ref[...].astype(F32), rb_ref[...].astype(F32)
    sides = jnp.where(at < 64, jnp.where(even, b, a), jnp.where(even, a, b))
    half = views // 2
    for c in range(3):
        side = pltpu.roll(sides, (-HALO * c) % LANES, 1)
        joined = jnp.where(from_left | from_right, side, strip_ref[c])
        x[c, :, 0:LANES] = joined[0 : x.shape[1], :]
        x[c, :, LANES:] = joined[half : half + x.shape[1], :]
    inside = jnp.concatenate([inside, inside], axis=1)
    first_layer(lambda c, at: x[c, :, at], half + 4, w1, a1, s1, s2, 0, inside)
    second_layer(half + 2, w2, a2, s2, s3, 0, inside)
    last_layer(half, a1.shape[0], w3, s3, update)
    strip = x[0, HALO : HALO + half, :] + update[...]
    strip = jnp.concatenate([strip[:, 0:LANES], strip[:, LANES:]], axis=0)
    first = iota((views, LANES), 1)
    for r in range(rows):
        head = main_ref[:, r * cols : r * cols + LANES]
        tail = main_ref[:, (r + 1) * cols - LANES : (r + 1) * cols]
        moved = pltpu.roll(strip, (-(16 * r + HALO)) % LANES, 1)
        head = jnp.where(first < HALO, moved, head)
        moved = pltpu.roll(strip, (LANES - HALO - (64 + 16 * r + HALO)) % LANES, 1)
        tail = jnp.where(first >= LANES - HALO, moved, tail)
        for t in range(cols // LANES):
            middle = main_ref[:, r * cols + t * LANES : r * cols + (t + 1) * LANES]
            last = cols // LANES - 1
            flat[t, pl.ds(r, views, stride=rows), :] = head if t == 0 else tail if t == last else middle
    per = 16 // rows
    owner = lax.broadcasted_iota(jnp.int32, (16, foot_ref.shape[1]), 0) // rows
    for q in range(views // per):
        block = jnp.concatenate([flat[t, 16 * q : 16 * q + 16, :] for t in range(cols // LANES)], axis=1).astype(BF16)
        dual_ref[16 * q : 16 * q + 16, :] = block
        got = None
        for i in range(per):
            one = lax.dot_general(
                block, foot_ref[q * per + i], (((1,), (1,)), ((), ())), preferred_element_type=F32
            )
            got = one if got is None else jnp.where(owner == i, one, got)
        back[16 * q : 16 * q + 16, :] = got.astype(BF16)
    partial = jnp.dot(axial_ref[...], back[...], preferred_element_type=F32)
    if len(parts) > 1:
        part_s[...] = partial
        cap = parts[0].shape[0]
        for k in range(n):
            parts[k][...] = part_s[pl.ds(pl.multiple_of(partner(n, True, k) * cap, cap), cap), :]
    else:
        parts[0][...] = partial


def shards(
    volume,
    requests,
    counts,
    axial,
    footprint,
    dual,
    measured,
    conv_first,
    slopes_first,
    conv_second,
    slopes_second,
    conv_last,
):
    n = lax.axis_size("view")
    slots = requests.shape[2]
    tiles, vox = volume.shape
    views, rows, cols = dual.shape
    wide = rows * cols
    channels = conv_second.shape[2]
    split = n in (2, 4)
    dma = pltpu.SemaphoreType.DMA
    pieces = [shape((slots, vox), BF16)] * n if split else [shape((n * slots, vox), BF16)]
    outgoing = call(
        functools.partial(gather_kernel, n, slots, split),
        pieces,
        [
            pltpu.VMEM(requests.shape, jnp.int32),
            pltpu.VMEM(counts.shape, jnp.int32),
            pltpu.VMEM(volume.shape, BF16),
            dma((3,)),
        ],
        from_hbm([requests, counts, volume]),
        [HBM] * 3,
    )
    incoming = exchange(outgoing, "view")

    small = [
        dual,
        measured,
        axial,
        conv_first.transpose(0, 1, 3, 2),
        conv_second,
        conv_last.reshape(3, 3, channels),
        slopes_first.reshape(1, channels),
        slopes_second.reshape(1, channels),
        requests,
        counts,
    ]
    flat = pltpu.VMEM((cols // LANES, views * rows, LANES), F32)
    full = (STEP + 2) * channels
    stat, foot, axial_flat, axial_back, w1, w2, w3, a1, a2, hot = call(
        functools.partial(setup_kernel, n, split),
        [
            shape((2, views, wide)),
            shape(footprint.shape, BF16),
            shape((views * rows, n * slots), BF16),
            shape((n * slots, views * rows), BF16),
            shape((BAND * channels, 144), BF16),
            shape((STEP * channels, 3 * full), BF16),
            shape((24, full), BF16),
            shape((channels, LANES)),
            shape((channels, LANES)),
            shape((tiles, n * slots), BF16),
        ],
        [
            dma((len(small) + 1,)),
            flat,
            pltpu.VMEM((views * rows, -(-n * slots // LANES) * LANES), F32),
            *[pltpu.VMEM(x.shape, x.dtype) for x in small],
        ],
        from_hbm([*small, footprint]),
        [HBM] * (len(small) + 1),
        cost=(10**8, 4 * 10**6),
    )

    message_rows = -(-9 * (wide // LANES) // 16) * 16
    edge = shape((message_rows, LANES), BF16)
    halo = pltpu.VMEM((2, message_rows, LANES), F32)
    slot_rows, edge_a, edge_b, ends = call(
        functools.partial(edge_kernel, n, rows),
        [shape((n * slots, vox), BF16), edge, edge, shape((cols // LANES, 32, LANES))],
        [halo],
        [axial_flat, foot, stat, *incoming],
    )
    halo_a, halo_b = both_ways(edge_a, edge_b, "view")
    fw = call(
        functools.partial(forward_kernel, rows),
        shape((views, wide)),
        [flat],
        [axial_flat, foot, slot_rows, ends],
        cost=(10**6, 10**4),
    )
    strip_msg = call(
        functools.partial(own_message_kernel, rows),
        shape((views, LANES)),
        [],
        [fw, stat],
        cost=(10**6, 10**4),
    )
    padded = 48
    message = call(
        functools.partial(strip_message_kernel, rows, cols // LANES),
        shape((padded, LANES), BF16),
        [pltpu.VMEM((padded, LANES), F32), halo],
        [strip_msg, halo_a, halo_b],
    )
    side_a, side_b = both_ways(message, message, "col")

    def net_scratch(count, width, one=None, *lead):
        one = one or count + 4
        return [
            pltpu.VMEM((*lead, 9, -(-one // BAND) * BAND + BAND, width), F32),
            pltpu.VMEM((*lead, 3, (count + 4) * channels, width), BF16),
            pltpu.VMEM((*lead, (count + 2) * channels, width), BF16),
            pltpu.VMEM((*lead, count, width), F32),
        ]

    weights = [w1, w2, w3, a1, a2]
    count = views - 2 * HALO
    one, two = call(
        inner_kernel,
        [shape((4 * channels, wide), BF16), shape(((count + 2) * channels, wide), BF16)],
        [pltpu.VMEM((3, views + BAND, wide), F32), *net_scratch(count, wide)[:2]],
        [fw, stat, w1, w2, a1, a2],
        cost=(10**6, 10**4),
    )
    main, strip = call(
        functools.partial(outer_kernel, rows),
        [shape((views, wide)), shape((3, padded, LANES))],
        [
            pltpu.VMEM((2, 3, 2 * BAND, wide), F32),
            halo,
            *net_scratch(HALO, wide, HALO, 2),
            pltpu.VMEM((count, wide), F32),
        ],
        [fw, stat, halo_a, halo_b, one, two, *weights],
        cost=(4 * 10**8, 2 * 10**6),
    )
    parts = [shape((slots, vox))] * n if split else [shape((n * slots, vox))]
    dual_out, *returned = call(
        functools.partial(back_kernel, n, rows),
        [shape((views * rows, cols), BF16), *parts],
        [
            pltpu.VMEM((3, padded - views // 2, 2 * LANES), F32),
            *net_scratch(views // 2, 2 * LANES),
            flat,
            pltpu.VMEM((views * rows, vox), BF16),
            pltpu.VMEM((n * slots, vox), F32),
        ],
        [strip, side_a, side_b, *weights, main, foot, axial_back],
    )
    arrived = exchange(returned, "view")
    backprojection = call(scatter_kernel, shape((tiles, vox)), [], [hot, *arrived])
    return dual_out.reshape(views, rows, cols), backprojection


def solution(mesh):
    in_specs = (
        P(("groups", "view"), "col"),
        P(("groups", "view"), None, None),
        P(("groups", "view"), None),
        P("view", None, None),
        P("view", None, "col"),
        P(("groups", "view"), None, "col"),
        P(("groups", "view"), None, "col"),
        P(),
        P(),
        P(),
        P(),
        P(),
    )
    out_specs = (P(("groups", "view"), None, "col"), P(("groups", "view"), "col"))
    return jax.shard_map(shards, mesh=mesh, in_specs=in_specs, out_specs=out_specs, check_vma=False)
```
